512 devices in a mesh: dp: 16 (over y, core), space: 32 (over z, x).
Axes of the slice: x: 4, y: 8, z: 8, core: 2. Of those that a mesh axis runs over, the one named last changes fastest.
Arguments:
- clips: bfloat16 [16, 1024, 9, 2, 4, 128], P('dp', 'space'), may hold values from -6 to 6
- a_tile: int32 [16, 1024], P('dp', 'space'), may hold values from 0 to 512, as said below
- gamma: float32 [128], replicated, may hold values from 0.1 to 1.9
- weight: bfloat16 [3456, 256], replicated, may hold values from -0.109375 to 0.109375
- cotangent: bfloat16 [16, 9, 32, 32, 256], P('dp', None, 'space'), may hold values from -6 to 6
Outputs:
- output: bfloat16 [16, 9, 32, 32, 256], P('dp', None, 'space')
- grad_input: bfloat16 [16, 1024, 9, 2, 4, 128], P('dp', 'space')
- grad_weight: float32 [3456, 256], P('space')
The draws below stay inside these ranges and needn't reach their ends.
Inputs may be any that keep to these rules, and one draw needn't show every extreme that they name: `a_tile`: each of a clip's 512 tiles is held by exactly one slot; every other slot holds 512. One device's 32 slots, in every draw, hold between 8 and 32 tiles, some device all 32; among one device's tiles at most 1 have the same t // 16, and this many is reached in every draw.
All inputs are finite; a program needn't handle non-finite values.
Results may differ from the reference program's by a relative error of at most 0.0049.
Values may be sent and summed in bfloat16 or wider, within the bound.
A program may use at most 64 MiB of HBM per device.

```python
import jax
import jax.numpy as jnp
import numpy as np
from jax import lax

C = 128
CO = 256
FR = 9
TC = 4
TPD = 16
CAP = 32
SLOTS = 1024
TILES = 512
WO = 32
CLIPS = 16
N_SPACE = 32


def draw_a_tile(key, part):
    key = jax.random.fold_in(key, 7)
    quarter = N_SPACE // 4
    counts = [2 * TPD] * quarter + [TPD] * quarter + [TPD // 2] * (N_SPACE - 2 * quarter)
    target_row = np.zeros((N_SPACE, CAP), np.int32)
    target_round = np.zeros((N_SPACE, CAP), np.int32)
    live_table = np.zeros((N_SPACE, CAP), np.int32)
    position = 0
    for owner in range(N_SPACE):
        for slot in range(counts[owner]):
            target_row[owner, slot] = position % N_SPACE
            target_round[owner, slot] = position // N_SPACE
            live_table[owner, slot] = 1
            position = position + 1

    def one_clip(clip_key):
        key_dev, key_col, key_slot = jax.random.split(clip_key, 3)
        col_orders = jax.vmap(lambda inner: jax.random.permutation(inner, TPD))(jax.random.split(key_col, N_SPACE))
        rows_tab = jnp.asarray(target_row)
        rounds_tab = jnp.asarray(target_round)
        numbers = rows_tab * TPD + col_orders[rows_tab, rounds_tab]
        numbers = jnp.where(jnp.asarray(live_table) > 0, numbers, TILES)
        slot_orders = jax.vmap(lambda inner: jax.random.permutation(inner, CAP))(jax.random.split(key_slot, N_SPACE))
        numbers = jnp.take_along_axis(numbers, slot_orders, axis=1)
        device_order = jax.random.permutation(key_dev, N_SPACE)
        placed = jnp.zeros_like(numbers).at[device_order].set(numbers)
        return placed.reshape(-1)
    return jax.vmap(one_clip)(jax.random.split(key, CLIPS)).astype(jnp.int32)


def level_of(key, shape, cuts, least, high):
    def one(dim, shards_of):
        draws = jax.random.uniform(jax.random.fold_in(jax.random.fold_in(key, 6), dim), (shards_of,), jnp.float32, least / len(cuts), high / len(cuts))
        return jnp.repeat(jnp.exp(draws), shape[dim] // shards_of).reshape((-1,) + (1,) * (len(shape) - dim - 1))

    loudness = one(*cuts[0])
    for cut in cuts[1:]:
        loudness = loudness * one(*cut)
    return loudness


def scatter_about(stream_key, dims, scale, limit, cuts=(), held_as=jnp.bfloat16):
    drawn = jax.random.normal(stream_key, dims, jnp.float32) * scale
    if len(cuts) > 0:
        drawn = level_of(stream_key, dims, cuts, -0.22, 0.18) * drawn
    return jnp.clip(drawn, min=-limit, max=limit).astype(held_as)


def setup_inputs(seed: int = 0) -> dict:
    key_list = jax.random.split(jax.random.key(seed), 6)
    return {
        "clips": scatter_about(key_list[0], (CLIPS, SLOTS, FR, 2, TC, C), 1.0, 6.0, ((0, 16), (1, 32))),
        "a_tile": draw_a_tile(jax.random.fold_in(key_list[5], 71), 0),
        "gamma": jnp.clip(1.0 + 0.18 * jax.random.normal(key_list[2], (C,), jnp.float32), 0.1, 1.9),
        "weight": scatter_about(key_list[3], (27 * C, CO), (27 * C) ** -0.5, 0.109375),
        "cotangent": scatter_about(key_list[4], (CLIPS, FR, N_SPACE, WO, CO), 1.0, 6.0, ((0, 16), (2, 32))),
    }


def activate(values, gamma):
    meansq = lax.optimization_barrier(jnp.mean(values * values, axis=-1, keepdims=True))
    normed = values * lax.rsqrt(meansq + 1e-06) * gamma.astype(jnp.float32)
    return jax.nn.silu(normed)

def tapped(padded, frames, rows_out, cols_out):
    pieces = []
    for frame_tap in range(3):
        for row_tap in range(3):
            for col_tap in range(3):
                pieces.append(padded[frame_tap:frame_tap + frames, row_tap:row_tap + 2 * rows_out - 1:2, col_tap:col_tap + 2 * cols_out - 1:2])
    return jnp.concatenate(pieces, axis=-1)

def spread(grad_taps, width):
    total = jnp.zeros((), jnp.float32)
    for frame_tap in range(3):
        for row_tap in range(3):
            for col_tap in range(3):
                piece = grad_taps[:, :, :, frame_tap, row_tap, col_tap]
                total = total + lax.pad(piece, jnp.zeros((), piece.dtype), ((frame_tap, 2 - frame_tap, 0), (row_tap, 2 - row_tap, 1), (col_tap, 2 - col_tap, 1), (0, 0, 0)))
    return total[2:, :-1, :width]

def reference(clips, a_tile, gamma, weight, cotangent):
    width = TPD * TC

    def one_clip(items):
        tile_slots, owners, grad_out = items
        tiles = jnp.zeros((TILES,) + tile_slots.shape[1:], jnp.bfloat16).at[owners].set(tile_slots, mode='drop')
        slab = tiles.reshape(N_SPACE, TPD, FR, 2, TC, C).transpose(2, 0, 3, 1, 4, 5).reshape(FR, 2 * N_SPACE, width, C)
        slab_f = slab.astype(jnp.float32)
        hidden = activate(slab_f, gamma).astype(jnp.bfloat16)
        padded = jnp.pad(hidden, ((2, 0), (0, 1), (0, 1), (0, 0)))
        patches = tapped(padded, FR, N_SPACE, WO).reshape(-1, 27 * C)
        result = jnp.dot(patches, weight, preferred_element_type=jnp.float32).astype(jnp.bfloat16)
        grad_rows = grad_out.reshape(-1, CO)
        weight_part = jnp.dot(patches.T, grad_rows, preferred_element_type=jnp.float32)
        grad_patch = jnp.dot(grad_rows, weight.T, preferred_element_type=jnp.float32)
        grad_patch = grad_patch.reshape(FR, N_SPACE, WO, 3, 3, 3, C)
        grad_hidden = spread(grad_patch, width).astype(jnp.bfloat16)
        pull = jax.vjp(lambda values: activate(values, gamma), slab_f)[1]
        grad_slab = pull(grad_hidden.astype(jnp.float32))[0].astype(jnp.bfloat16)
        grad_tiles = grad_slab.reshape(FR, N_SPACE, 2, TPD, TC, C).transpose(1, 3, 0, 2, 4, 5).reshape(TILES, FR, 2, TC, C)
        live = owners < TILES
        picked = jnp.take(grad_tiles, jnp.minimum(owners, TILES - 1).astype(jnp.int32), axis=0)
        picked = jnp.where(live[:, None, None, None, None], picked, jnp.zeros((), jnp.bfloat16))
        return (result.reshape(FR, N_SPACE, WO, CO), picked, weight_part)
    outputs, grads, weight_parts = lax.map(one_clip, (clips, a_tile, cotangent))
    return (outputs, grads, lax.optimization_barrier(jnp.sum(weight_parts, axis=0)))
```

```python
import functools

import jax
import jax.numpy as jnp
from jax import lax
from jax.experimental import pallas as pl
from jax.experimental.pallas import tpu as pltpu
from jax.sharding import PartitionSpec as P

TPD = 16
BF = jnp.bfloat16
F32 = jnp.float32
NN = (((1,), (0,)), ((), ()))
NT = (((1,), (1,)), ((), ()))
TN = (((0,), (0,)), ((), ()))


def remote(src, dst, ssem, rsem, dev):
    return pltpu.make_async_remote_copy(
        src_ref=src,
        dst_ref=dst,
        send_sem=ssem,
        recv_sem=rsem,
        device_id=dev,
        device_id_type=pl.DeviceIdType.MESH,
    )


def loop(lo, hi, body, unroll=1):
    def step(i, carry):
        body(i)
        return carry

    lax.fori_loop(lo, hi, step, 0, unroll=unroll)


def normed(x):
    meansq = jnp.mean(x * x, axis=-1, keepdims=True)
    scale = lax.rsqrt(meansq + 1e-06)
    return x * scale, scale


def kernel(
    dims,
    slot_of,
    owners,
    locs,
    clips_h,
    gamma,
    weight_h,
    cot_h,
    out,
    gin,
    fin,
    clips,
    weight,
    cot,
    cotprev,
    stage,
    arr,
    stage2,
    ret,
    locr,
    map_v,
    map_s,
    tile32,
    tiles,
    planes,
    xmat,
    gmat,
    cs,
    cr,
    cws,
    cwr,
    ccs,
    ccr,
    spst,
    spr,
    finr,
    in_sem,
    id_s,
    id_r,
    st_s,
    st_r,
    rt_s,
    rt_r,
    hop_s,
    hop_r,
    core_s,
    core_r,
    cw_s,
    cw_r,
    cc_s,
    cc_r,
    sp_s,
    sp_r,
    ag_s,
    ag_r,
):
    ns, ny, frames, half, wrows, rc = dims
    ndp = 2 * ny
    chans = 128
    tpd = half // 2
    me = lax.axis_index("space")
    dp = lax.axis_index("dp")
    y = dp // 2
    core = lax.rem(dp, 2)
    fj = frames * half

    def begin(k):
        return ((k * wrows) // 16) * 16

    loads = [
        pltpu.make_async_copy(clips_h, clips, in_sem.at[0]),
        pltpu.make_async_copy(cot_h, cot, in_sem.at[1]),
        pltpu.make_async_copy(weight_h, weight, in_sem.at[2]),
    ]
    for load in loads:
        load.start()
    barrier = pltpu.get_barrier_semaphore()

    def greet_space(i):
        pl.semaphore_signal(
            barrier,
            inc=1,
            device_id={"space": lax.rem(me + i, ns)},
            device_id_type=pl.DeviceIdType.MESH,
        )

    def greet_dp(i):
        pl.semaphore_signal(
            barrier,
            inc=1,
            device_id={"dp": lax.rem(dp + i, ndp)},
            device_id_type=pl.DeviceIdType.MESH,
        )

    loop(1, ns, greet_space)
    loop(1, ndp, greet_dp)

    @pl.when(me == 0)
    def _():
        cotprev[...] = jnp.zeros(cotprev.shape, BF)

    @pl.when(me == ns - 1)
    def _():
        xmat[:, 6 * chans : 8 * chans] = jnp.zeros((fj, 2 * chans), BF)

    gmat[:, 27 * chans :, :] = jnp.zeros((2, gmat.shape[1] - 27 * chans, 128), F32)
    gam = gamma[...]
    loads[0].wait()
    loads[1].wait()
    pl.semaphore_wait(barrier, ns - 1 + ndp - 1)

    def id_copy(d, s):
        return remote(locs.at[d], locr.at[s], id_s.at[d], id_r.at[s], {"space": d})

    def send_ids(i):
        id_copy(lax.rem(me + i, ns), me).start()

    loop(1, ns, send_ids)
    locr[me] = locs[me]

    above = lax.rem(me + ns - 1, ns)
    under = lax.rem(me + 1, ns)
    cot_copy = remote(cot, cotprev, hop_s.at[0], hop_r.at[0], {"space": under})
    row_copy = remote(
        xmat.at[:, 0 : 2 * chans],
        xmat.at[:, 6 * chans : 8 * chans],
        hop_s.at[1],
        hop_r.at[1],
        {"space": above},
    )

    @pl.when(me < ns - 1)
    def _():
        cot_copy.start()

    def hidden_of(d):
        n, _ = normed(clips[slot_of[d]].astype(F32))
        v = n * gam
        return (v / (1.0 + jnp.exp(-v))).astype(BF)

    def tile_copy(d, s):
        return remote(stage.at[d], arr.at[s], st_s.at[d], st_r.at[s], {"space": d})

    def send_tile(i):
        d = lax.rem(me + i, ns)
        stage[d] = hidden_of(d)
        tile_copy(d, me).start()

    loop(1, ns, send_tile)
    arr[me] = hidden_of(me)

    loads[2].wait()

    @pl.when(me > 0)
    def _():
        cot_copy.wait_recv()

    colrow = lax.rem(lax.broadcasted_iota(jnp.int32, (fj, chans), 0), half)

    def wpart(a, b):
        return weight[pl.ds((a * 9 + b * 3) * chans, 3 * chans), :]

    def back(source, b):
        total = lax.dot_general(source[...], wpart(2, b), NT, preferred_element_type=F32)
        for a in (1, 0):
            skip = (2 - a) * half
            part = lax.dot_general(
                source[skip:, :], wpart(a, b), NT, preferred_element_type=F32
            )
            total = total + jnp.concatenate(
                [part, jnp.zeros((skip, 3 * chans), F32)], axis=0
            )
        return total

    def put_planes(total, b):
        moved = pltpu.roll(total[:, 2 * chans :], 1, 0)
        moved = jnp.where(colrow == 0, 0.0, moved)
        planes[2 * b] = total[:, :chans] + moved
        planes[2 * b + 1] = total[:, chans : 2 * chans]

    put_planes(back(cot, 0) + back(cotprev, 2), 0)
    put_planes(back(cot, 1), 1)

    def cut_tile(t):
        for b in range(2):
            for par in range(2):
                for jj in range(2):
                    tile32[t, pl.ds(b * 4 + jj * 2 + par, frames, stride=8), :] = planes[
                        2 * b + par, pl.ds(2 * t + jj, frames, stride=half), :
                    ]
        tiles[t] = tile32[t].astype(BF)

    loop(0, tpd, cut_tile)

    def wait_id(i):
        id_copy(lax.rem(me + i, ns), lax.rem(me + i, ns)).wait_recv()

    loop(1, ns, wait_id)
    got = locr[:, 0, :]
    lane = lax.broadcasted_iota(jnp.int32, (ns, 128), 1)
    who = lax.broadcasted_iota(jnp.int32, (ns, 128), 0)
    src_of = jnp.max(jnp.where(got == lane, who, 0), axis=0, keepdims=True)
    map_v[0:ns, :] = got
    map_v[ns : ns + 8, :] = jnp.broadcast_to(src_of, (8, 128))
    to_scalar = pltpu.make_async_copy(map_v, map_s, in_sem.at[3])
    to_scalar.start()
    to_scalar.wait()

    def wait_tile(i):
        tile_copy(lax.rem(me + i, ns), lax.rem(me + i, ns)).wait_recv()

    loop(1, ns, wait_tile)

    def lay_tile(t):
        tile32[t] = arr[map_s[ns, t]].astype(F32)
        for b in range(2):
            for par in range(2):
                for jj in range(2):
                    planes[2 * b + par, pl.ds(2 * t + jj, frames, stride=half), :] = tile32[
                        t, pl.ds(b * 4 + jj * 2 + par, frames, stride=8), :
                    ]

    loop(0, tpd, lay_tile)

    def next_col(even):
        return jnp.where(colrow == half - 1, 0.0, pltpu.roll(even, fj - 1, 0)).astype(BF)

    for b in range(2):
        even = planes[2 * b]
        xmat[:, (3 * b) * chans : (3 * b + 1) * chans] = even.astype(BF)
        xmat[:, (3 * b + 1) * chans : (3 * b + 2) * chans] = planes[2 * b + 1].astype(BF)
        xmat[:, (3 * b + 2) * chans : (3 * b + 3) * chans] = next_col(even)

    @pl.when(me > 0)
    def _():
        row_copy.start()

    def back_copy(d, s):
        return remote(stage2.at[d], ret.at[s], rt_s.at[d], rt_r.at[s], {"space": d})

    def send_back(i):
        d = lax.rem(me + i, ns)
        stage2[d] = tiles[jnp.maximum(map_s[d, 0], 0)]
        back_copy(d, me).start()

    loop(1, ns, send_back)
    ret[me] = tiles[jnp.maximum(map_s[me, 0], 0)]

    def weight_grad(b):
        for a in range(3):
            count = fj - (2 - a) * half
            part = lax.dot_general(
                xmat[0:count, 3 * b * chans : 3 * (b + 1) * chans],
                cot[fj - count :, :],
                TN,
                preferred_element_type=F32,
            )
            row = (9 * a + 3 * b) * chans
            gmat[0, row : row + 3 * chans, :] = part[:, :128]
            gmat[1, row : row + 3 * chans, :] = part[:, 128:]

    weight_grad(1)
    weight_grad(0)

    @pl.when(me < ns - 1)
    def _():
        row_copy.wait_recv()

    xmat[:, 8 * chans : 9 * chans] = next_col(
        xmat[:, 6 * chans : 7 * chans].astype(F32)
    )
    weight_grad(2)

    other = {"dp": 2 * y + 1 - core}

    def core_copy(k):
        return remote(cs.at[k], cr.at[k], core_s.at[k], core_r.at[k], other)

    reach = ny // 2
    order = []
    for i in range(reach):
        order.append(reach - i)
        if i < reach - 1:
            order.append(ny - (reach - 1 - i))
    order.append(0)

    for off in order:
        k = lax.rem(y + off, ny)

        def pack(s, k=k):
            row = pl.multiple_of(begin(s) + rc * k, 16)
            cs[k, s] = gmat[1 - core, pl.ds(row, rc), :].astype(BF)

        loop(0, ns, pack)
        core_copy(k).start()

    total = lax.dot_general(xmat[...], weight[18 * chans :, :], NN, preferred_element_type=F32)
    for a in (1, 0):
        skip = (2 - a) * half
        part = lax.dot_general(
            xmat[0 : fj - skip, :],
            weight[9 * a * chans : 9 * (a + 1) * chans, :],
            NN,
            preferred_element_type=F32,
        )
        total = total + jnp.concatenate([jnp.zeros((skip, 256), F32), part], axis=0)
    out[...] = total.astype(BF)

    def mine(k, s):
        row = pl.multiple_of(begin(s) + rc * k, 16)
        return gmat[core, pl.ds(row, rc), :] + cr[k, s].astype(F32)

    up = {"dp": 2 * lax.rem(y + 1, ny) + core}
    down = {"dp": 2 * lax.rem(y + ny - 1, ny) + core}
    for i in range(reach):
        k = lax.rem(y + reach - i, ny)
        core_copy(k).wait_recv()
        if i > 0:
            remote(cws.at[i - 1], cwr.at[i - 1], cw_s.at[i - 1], cw_r.at[i - 1], up).wait_recv()

        def add_up(s, k=k, i=i):
            v = mine(k, s)
            if i > 0:
                v = v + cwr[i - 1, s].astype(F32)
            cws[i, s] = v.astype(BF)

        loop(0, ns, add_up)
        remote(cws.at[i], cwr.at[i], cw_s.at[i], cw_r.at[i], up).start()
        if i < reach - 1:
            k = lax.rem(y + ny - (reach - 1 - i), ny)
            core_copy(k).wait_recv()
            if i > 0:
                remote(
                    ccs.at[i - 1], ccr.at[i - 1], cc_s.at[i - 1], cc_r.at[i - 1], down
                ).wait_recv()

            def add_down(s, k=k, i=i):
                v = mine(k, s)
                if i > 0:
                    v = v + ccr[i - 1, s].astype(F32)
                ccs[i, s] = v.astype(BF)

            loop(0, ns, add_down)
            remote(ccs.at[i], ccr.at[i], cc_s.at[i], cc_r.at[i], down).start()

    core_copy(y).wait_recv()
    remote(
        cws.at[reach - 1], cwr.at[reach - 1], cw_s.at[reach - 1], cw_r.at[reach - 1], up
    ).wait_recv()
    if reach > 1:
        remote(
            ccs.at[reach - 2], ccr.at[reach - 2], cc_s.at[reach - 2], cc_r.at[reach - 2], down
        ).wait_recv()

    def sp_copy(d, s):
        return remote(spst.at[d], spr.at[s], sp_s.at[d], sp_r.at[s], {"space": d})

    def chunk_sum(s):
        v = mine(y, s) + cwr[reach - 1, s].astype(F32)
        if reach > 1:
            v = v + ccr[reach - 2, s].astype(F32)
        return v.astype(BF)

    def send_sp(i):
        d = lax.rem(me + i, ns)
        spst[d] = chunk_sum(d)
        sp_copy(d, me).start()

    loop(1, ns, send_sp)
    spr[me] = chunk_sum(me)

    def wait_back(i):
        back_copy(lax.rem(me + i, ns), lax.rem(me + i, ns)).wait_recv()

    loop(1, ns, wait_back)

    def pull(k):
        tile = owners[k]
        g = ret[jnp.minimum(tile // tpd, ns - 1)].astype(F32)
        g = jnp.where(tile < tpd * ns, g, 0.0)
        n, scale = normed(clips[k].astype(F32))
        v = n * gam
        sig = 1.0 / (1.0 + jnp.exp(-v))
        dn = g * sig * (1.0 + v * (1.0 - sig)) * gam
        gin[k] = (scale * (dn - n * jnp.mean(dn * n, axis=-1, keepdims=True))).astype(BF)

    loop(0, ns, pull)

    def wait_sp(i):
        sp_copy(lax.rem(me + i, ns), lax.rem(me + i, ns)).wait_recv()

    loop(1, ns, wait_sp)
    finr[core, y] = jnp.sum(spr[...].astype(F32), axis=0)

    def ag_copy(d, s):
        slot = finr.at[lax.rem(s, 2), s // 2]
        return remote(slot, slot, ag_s.at[d], ag_r.at[s], {"dp": d})

    def send_ag(i):
        ag_copy(lax.rem(dp + i, ndp), dp).start()

    loop(1, ndp, send_ag)

    def wait_ag(i):
        d = lax.rem(dp + i, ndp)
        ag_copy(d, d).wait_recv()

    loop(1, ndp, wait_ag)
    for h in range(2):
        for k in range(ny):
            fin[h, k * rc : (k + 1) * rc, :] = finr[h, k]

    def done_space(i):
        d = lax.rem(me + i, ns)
        id_copy(d, me).wait_send()
        tile_copy(d, me).wait_send()
        back_copy(d, me).wait_send()
        sp_copy(d, me).wait_send()

    loop(1, ns, done_space)

    def done_dp(i):
        ag_copy(lax.rem(dp + i, ndp), dp).wait_send()

    loop(1, ndp, done_dp)

    def done_core(k):
        core_copy(k).wait_send()

    loop(0, ny, done_core)
    for i in range(reach):
        remote(cws.at[i], cwr.at[i], cw_s.at[i], cw_r.at[i], up).wait_send()
    for i in range(reach - 1):
        remote(ccs.at[i], ccr.at[i], cc_s.at[i], cc_r.at[i], down).wait_send()

    @pl.when(me < ns - 1)
    def _():
        cot_copy.wait_send()

    @pl.when(me > 0)
    def _():
        row_copy.wait_send()


def local(clips, a_tile, gamma, weight, cotangent):
    ns = lax.axis_size("space")
    ny = lax.axis_size("dp") // 2
    me = lax.axis_index("space")
    frames, rows_in, tcols, chans = clips.shape[2:]
    half = cotangent.shape[3]
    tpd = half // 2
    cap = clips.shape[1]
    fj = frames * half
    trows = frames * rows_in * tcols
    wrows = weight.shape[0] // ns
    rc = 16 * -(-(wrows + 12) // (16 * ny))
    pad = max(((s * wrows) // 16) * 16 + rc * ny for s in range(ns))
    owners = a_tile[0]
    match = (owners // tpd)[None, :] == jnp.arange(ns)[:, None]
    slot_of = jnp.max(jnp.where(match, jnp.arange(cap)[None, :], 0), axis=1)
    col = jnp.max(jnp.where(match, (owners % tpd)[None, :], -1), axis=1)
    locs = jnp.broadcast_to(col[:, None, None], (ns, 8, 128))
    vmem = pl.BlockSpec(memory_space=pltpu.VMEM)
    smem = pl.BlockSpec(memory_space=pltpu.SMEM)
    hbm = pl.BlockSpec(memory_space=pl.ANY)
    dma = pltpu.SemaphoreType.DMA
    tiles_shape = pltpu.VMEM((ns, trows, chans), BF)
    reach = ny // 2
    piece = (ns, rc, 128)
    out, gin, fin = pl.pallas_call(
        functools.partial(kernel, (ns, ny, frames, half, wrows, rc)),
        out_shape=(
            jax.ShapeDtypeStruct((fj, 256), BF),
            jax.ShapeDtypeStruct((cap, trows, chans), BF),
            jax.ShapeDtypeStruct((2, rc * ny, 128), F32),
        ),
        in_specs=[smem, smem, vmem, hbm, vmem, hbm, hbm],
        out_specs=(vmem, vmem, vmem),
        scratch_shapes=[
            pltpu.VMEM((cap, trows, chans), BF),
            pltpu.VMEM(weight.shape, BF),
            pltpu.VMEM((fj, 256), BF),
            pltpu.VMEM((fj, 256), BF),
            tiles_shape,
            tiles_shape,
            tiles_shape,
            tiles_shape,
            pltpu.VMEM((ns, 8, 128), jnp.int32),
            pltpu.VMEM((ns + 8, 128), jnp.int32),
            pltpu.SMEM((ns + 8, 128), jnp.int32),
            pltpu.VMEM((tpd, trows, chans), F32),
            pltpu.VMEM((tpd, trows, chans), BF),
            pltpu.VMEM((4, fj, chans), F32),
            pltpu.VMEM((fj, 9 * chans), BF),
            pltpu.VMEM((2, pad, 128), F32),
            pltpu.VMEM((ny,) + piece, BF),
            pltpu.VMEM((ny,) + piece, BF),
            pltpu.VMEM((reach,) + piece, BF),
            pltpu.VMEM((reach,) + piece, BF),
            pltpu.VMEM((max(reach - 1, 1),) + piece, BF),
            pltpu.VMEM((max(reach - 1, 1),) + piece, BF),
            pltpu.VMEM(piece, BF),
            pltpu.VMEM(piece, BF),
            pltpu.VMEM((2, ny, rc, 128), F32),
            dma((4,)),
            dma((ns,)),
            dma((ns,)),
            dma((ns,)),
            dma((ns,)),
            dma((ns,)),
            dma((ns,)),
            dma((2,)),
            dma((2,)),
            dma((ny,)),
            dma((ny,)),
            dma((reach,)),
            dma((reach,)),
            dma((reach,)),
            dma((reach,)),
            dma((ns,)),
            dma((ns,)),
            dma((2 * ny,)),
            dma((2 * ny,)),
        ],
        compiler_params=pltpu.CompilerParams(
            collective_id=0, has_side_effects=True, vmem_limit_bytes=48 * 1024 * 1024
        ),
    )(
        slot_of,
        owners,
        locs,
        clips.reshape(cap, trows, chans),
        gamma.reshape(1, chans),
        weight,
        cotangent.reshape(fj, 256),
    )
    both = jnp.concatenate([fin[0], fin[1]], axis=1)
    first = me * wrows
    grad_weight = lax.dynamic_slice_in_dim(both, first - (first // 16) * 16, wrows, 0)
    return (
        out.reshape(1, frames, 1, half, 256),
        gin.reshape(clips.shape),
        grad_weight,
    )


def solution(mesh):
    return jax.shard_map(
        local,
        mesh=mesh,
        in_specs=(
            P("dp", "space", None, None, None, None),
            P("dp", "space"),
            P(),
            P(),
            P("dp", None, "space", None, None),
        ),
        out_specs=(
            P("dp", None, "space", None, None),
            P("dp", "space", None, None, None, None),
            P("space", None),
        ),
        check_vma=False,
    )
```

```python
import functools

import jax
import jax.numpy as jnp
from jax import lax
from jax.experimental import pallas as pl
from jax.experimental.pallas import tpu as pltpu
from jax.sharding import PartitionSpec as P

TPD = 16
BF = jnp.bfloat16
F32 = jnp.float32
NN = (((1,), (0,)), ((), ()))
NT = (((1,), (1,)), ((), ()))
TN = (((0,), (0,)), ((), ()))


def remote(src, dst, ssem, rsem, dev):
    return pltpu.make_async_remote_copy(
        src_ref=src,
        dst_ref=dst,
        send_sem=ssem,
        recv_sem=rsem,
        device_id=dev,
        device_id_type=pl.DeviceIdType.MESH,
    )


def loop(lo, hi, body, unroll=1):
    def step(i, carry):
        body(i)
        return carry

    lax.fori_loop(lo, hi, step, 0, unroll=unroll)


def normed(x):
    meansq = jnp.mean(x * x, axis=-1, keepdims=True)
    scale = lax.rsqrt(meansq + 1e-06)
    return x * scale, scale


def kernel(
    dims,
    owners,
    ids,
    clips_h,
    gamma,
    weight_h,
    cot_h,
    out,
    gin,
    fin,
    clips,
    weight,
    cot,
    cotprev,
    hid,
    slot_v,
    slot_s,
    stage,
    arr,
    stage2,
    ret,
    locr,
    map_v,
    map_s,
    tile32,
    tiles,
    planes,
    grads,
    gown,
    gtile32,
    xmat,
    gmat,
    cs,
    cr,
    cws,
    cwr,
    ccs,
    ccr,
    spst,
    spr,
    finr,
    in_sem,
    id_s,
    id_r,
    st_s,
    st_r,
    rt_s,
    rt_r,
    hop_s,
    hop_r,
    core_s,
    core_r,
    cw_s,
    cw_r,
    cc_s,
    cc_r,
    sp_s,
    sp_r,
    ag_s,
    ag_r,
):
    ns, nx, ny, frames, half, wrows, rc, flows = dims
    spans = [(f[0][0], f[-1][1]) for f in flows]
    ndp = 2 * ny
    chans = 128
    tpd = half // 2
    me = lax.axis_index("space")
    dp = lax.axis_index("dp")
    y = dp // 2
    core = lax.rem(dp, 2)
    fj = frames * half

    def begin(k):
        return ((k * wrows) // 16) * 16

    loads = [
        pltpu.make_async_copy(clips_h, clips, in_sem.at[0]),
        pltpu.make_async_copy(cot_h, cot, in_sem.at[1]),
        pltpu.make_async_copy(weight_h, weight, in_sem.at[2]),
    ]
    for load in loads:
        load.start()
    barrier = pltpu.get_barrier_semaphore()

    def greet_space(i):
        pl.semaphore_signal(
            barrier,
            inc=1,
            device_id={"space": lax.rem(me + i, ns)},
            device_id_type=pl.DeviceIdType.MESH,
        )

    def greet_dp(i):
        pl.semaphore_signal(
            barrier,
            inc=1,
            device_id={"dp": lax.rem(dp + i, ndp)},
            device_id_type=pl.DeviceIdType.MESH,
        )

    loop(1, ns, greet_space)
    loop(1, ndp, greet_dp)

    @pl.when(me == 0)
    def _():
        cotprev[...] = jnp.zeros(cotprev.shape, BF)

    @pl.when(me == ns - 1)
    def _():
        xmat[:, 6 * chans : 8 * chans] = jnp.zeros((fj, 2 * chans), BF)

    gmat[:, 27 * chans :, :] = jnp.zeros((2, gmat.shape[1] - 27 * chans, 128), F32)
    shape = (ns, 128)
    own_ids = jnp.broadcast_to(ids[...], shape)
    first_id = lax.broadcasted_iota(jnp.int32, shape, 0) * tpd
    match = (own_ids >= first_id) & (own_ids < first_id + tpd)
    slots = lax.broadcasted_iota(jnp.int32, shape, 1)
    slot_of = jnp.max(jnp.where(match, slots, 0), axis=1, keepdims=True)
    slot_of = jnp.minimum(slot_of, clips.shape[0] - 1)
    slot_v[...] = jnp.broadcast_to(slot_of, (ns, 128))
    locr[me] = ids[...]
    slot_copy = pltpu.make_async_copy(slot_v, slot_s, in_sem.at[4])
    slot_copy.start()

    gam = gamma[...]
    loads[0].wait()

    def hide(k):
        n, _ = normed(clips[k].astype(F32))
        v = n * gam
        hid[k] = (v / (1.0 + jnp.exp(-v))).astype(BF)

    loop(0, clips.shape[0], hide, 4)
    slot_copy.wait()

    def set_out(d):
        stage[d] = hid[slot_s[d, 0]]

    loop(0, ns, set_out, 4)
    arr[me] = stage[me]
    loads[1].wait()
    pl.semaphore_wait(barrier, ns - 1 + ndp - 1)

    zme = me // nx
    xme = lax.rem(me, nx)
    nz = ns // nx

    def id_x(d, s):
        return remote(
            locr.at[zme * nx + s], locr.at[zme * nx + s], id_s.at[d], id_r.at[s],
            {"space": zme * nx + d},
        )

    def id_z(d, s):
        rows = locr.at[pl.ds(s * nx, nx)]
        return remote(
            rows, rows, id_s.at[nx + d], id_r.at[nx + s], {"space": d * nx + xme}
        )

    def tile_copy(d, s):
        return remote(stage.at[d], arr.at[s], st_s.at[d], st_r.at[s], {"space": d})

    for i in range(1, nx):
        id_x(lax.rem(xme + i, nx), xme).start()

    above = lax.rem(me + ns - 1, ns)
    under = lax.rem(me + 1, ns)
    cot_copy = remote(cot, cotprev, hop_s.at[0], hop_r.at[0], {"space": under})
    row_copy = remote(
        xmat.at[:, 0 : 2 * chans],
        xmat.at[:, 6 * chans : 8 * chans],
        hop_s.at[1],
        hop_r.at[1],
        {"space": above},
    )

    def send_tile(i):
        tile_copy(lax.rem(me + i, ns), me).start()

    loop(1, ns, send_tile)

    @pl.when(me < ns - 1)
    def _():
        cot_copy.start()

    for i in range(1, nx):
        d = lax.rem(xme + i, nx)
        id_x(d, d).wait_recv()
    for i in range(1, nz):
        id_z(lax.rem(zme + i, nz), zme).start()

    loads[2].wait()
    colrow = lax.rem(lax.broadcasted_iota(jnp.int32, (fj, chans), 0), half)

    def wpart(a, b):
        return weight[pl.ds((a * 9 + b * 3) * chans, 3 * chans), :]

    def back(source, b):
        total = lax.dot_general(source[...], wpart(2, b), NT, preferred_element_type=F32)
        for a in (1, 0):
            skip = (2 - a) * half
            part = lax.dot_general(
                source[skip:, :], wpart(a, b), NT, preferred_element_type=F32
            )
            total = total + jnp.concatenate(
                [part, jnp.zeros((skip, 3 * chans), F32)], axis=0
            )
        return total

    def put_planes(total, b):
        moved = pltpu.roll(total[:, 2 * chans :], 1, 0)
        moved = jnp.where(colrow == 0, 0.0, moved)
        grads[2 * b] = total[:, :chans] + moved
        grads[2 * b + 1] = total[:, chans : 2 * chans]

    put_planes(back(cot, 1), 1)
    upper = back(cot, 0)
    gown[...] = upper

    for i in range(1, nz):
        d = lax.rem(zme + i, nz)
        id_z(d, d).wait_recv()
    every = locr[:, 0, :]
    low = me * tpd
    in_row = (every >= low) & (every < low + tpd)
    got = jnp.broadcast_to(
        jnp.max(jnp.where(in_row, every - low, -1), axis=1, keepdims=True), (ns, 128)
    )
    lane = lax.broadcasted_iota(jnp.int32, (ns, 128), 1)
    who = lax.broadcasted_iota(jnp.int32, (ns, 128), 0)
    src_of = jnp.max(jnp.where(got == lane, who, 0), axis=0, keepdims=True)
    map_v[0:ns, :] = got
    map_v[ns : ns + 8, :] = jnp.broadcast_to(src_of, (8, 128))
    to_scalar = pltpu.make_async_copy(map_v, map_s, in_sem.at[3])
    to_scalar.start()
    to_scalar.wait()

    def wait_tile(i):
        tile_copy(lax.rem(me + i, ns), lax.rem(me + i, ns)).wait_recv()

    loop(1, ns, wait_tile)

    def lay_tile(t):
        tile32[t] = arr[map_s[ns, t]].astype(F32)
        for b in range(2):
            for par in range(2):
                for jj in range(2):
                    planes[2 * b + par, pl.ds(2 * t + jj, frames, stride=half), :] = tile32[
                        t, pl.ds(b * 4 + jj * 2 + par, frames, stride=8), :
                    ]

    loop(0, tpd, lay_tile, 2)

    def next_col(even):
        return jnp.where(colrow == half - 1, 0.0, pltpu.roll(even, fj - 1, 0)).astype(BF)

    def put_rows(b):
        even = planes[2 * b]
        xmat[:, (3 * b) * chans : (3 * b + 1) * chans] = even.astype(BF)
        xmat[:, (3 * b + 1) * chans : (3 * b + 2) * chans] = planes[2 * b + 1].astype(BF)
        xmat[:, (3 * b + 2) * chans : (3 * b + 3) * chans] = next_col(even)

    put_rows(0)

    @pl.when(me > 0)
    def _():
        row_copy.start()

    put_rows(1)

    def weight_grad(b):
        for a in range(3):
            count = fj - (2 - a) * half
            part = lax.dot_general(
                xmat[0:count, 3 * b * chans : 3 * (b + 1) * chans],
                cot[fj - count :, :],
                TN,
                preferred_element_type=F32,
            )
            row = (9 * a + 3 * b) * chans
            gmat[0, row : row + 3 * chans, :] = part[:, :128]
            gmat[1, row : row + 3 * chans, :] = part[:, 128:]

    other = {"dp": 2 * y + 1 - core}

    def core_copy(k, f):
        lo, hi = spans[f]
        return remote(
            cs.at[k, lo:hi], cr.at[k, lo:hi], core_s.at[f, k], core_r.at[f, k], other
        )

    reach = ny // 2
    order = []
    for i in range(reach):
        order.append(reach - i)
        if i < reach - 1:
            order.append(ny - (reach - 1 - i))
    order.append(0)

    def each(f, body):
        for lo, hi, shift in flows[f]:
            loop(lo, hi, lambda q, shift=shift: body(q, q + shift))

    def send_core(f):
        def pack(q, s):
            row = pl.multiple_of(begin(s), 16)
            window = gmat[1 - core, pl.ds(row, rc * ny), :].astype(BF)
            cs[:, q] = window.reshape(ny, rc, 128)

        each(f, pack)
        for off in order:
            core_copy(lax.rem(y + off, ny), f).start()

    weight_grad(1)
    weight_grad(0)
    send_core(0)

    @pl.when(me > 0)
    def _():
        cot_copy.wait_recv()

    put_planes(gown[...] + back(cotprev, 2), 0)

    def cut_tile(t):
        for b in range(2):
            for par in range(2):
                for jj in range(2):
                    gtile32[t, pl.ds(b * 4 + jj * 2 + par, frames, stride=8), :] = grads[
                        2 * b + par, pl.ds(2 * t + jj, frames, stride=half), :
                    ]
        tiles[t] = gtile32[t].astype(BF)

    loop(0, tpd, cut_tile, 2)

    def back_copy(d, s):
        return remote(stage2.at[d], ret.at[s], rt_s.at[d], rt_r.at[s], {"space": d})

    def send_back(i):
        d = lax.rem(me + i, ns)
        stage2[d] = tiles[jnp.maximum(map_s[d, 0], 0)]
        back_copy(d, me).start()

    loop(1, ns, send_back)
    ret[me] = tiles[jnp.maximum(map_s[me, 0], 0)]

    @pl.when(me < ns - 1)
    def _():
        row_copy.wait_recv()

    xmat[:, 8 * chans : 9 * chans] = next_col(
        xmat[:, 6 * chans : 7 * chans].astype(F32)
    )
    weight_grad(2)
    send_core(1)

    def mine(k, q, s):
        row = pl.multiple_of(begin(s) + rc * k, 16)
        return gmat[core, pl.ds(row, rc), :] + cr[k, q].astype(F32)

    up = {"dp": 2 * lax.rem(y + 1, ny) + core}
    down = {"dp": 2 * lax.rem(y + ny - 1, ny) + core}

    def up_copy(i, f):
        lo, hi = spans[f]
        return remote(cws.at[i, lo:hi], cwr.at[i, lo:hi], cw_s.at[f, i], cw_r.at[f, i], up)

    def down_copy(i, f):
        lo, hi = spans[f]
        return remote(ccs.at[i, lo:hi], ccr.at[i, lo:hi], cc_s.at[f, i], cc_r.at[f, i], down)

    def hop(k, i, f, send, into, out_of):
        core_copy(k, f).wait_recv()
        if i > 0:
            send(i - 1, f).wait_recv()

        def add(q, s):
            v = mine(k, q, s)
            if i > 0:
                v = v + out_of[i - 1, q].astype(F32)
            into[i, q] = v.astype(BF)

        each(f, add)
        send(i, f).start()

    def chain(i):
        for f in range(2):
            hop(lax.rem(y + reach - i, ny), i, f, up_copy, cws, cwr)
            if i < reach - 1:
                hop(lax.rem(y + ny - (reach - 1 - i), ny), i, f, down_copy, ccs, ccr)

    chain(0)
    total = lax.dot_general(xmat[...], weight[18 * chans :, :], NN, preferred_element_type=F32)
    for a in (1, 0):
        skip = (2 - a) * half
        part = lax.dot_general(
            xmat[0 : fj - skip, :],
            weight[9 * a * chans : 9 * (a + 1) * chans, :],
            NN,
            preferred_element_type=F32,
        )
        total = total + jnp.concatenate([jnp.zeros((skip, 256), F32), part], axis=0)
    out[...] = total.astype(BF)

    for i in range(1, reach):
        chain(i)

    def sp_copy(d, s):
        return remote(spst.at[d], spr.at[s], sp_s.at[d], sp_r.at[s], {"space": d})

    def spread(q, s):
        v = mine(y, q, s) + cwr[reach - 1, q].astype(F32)
        if reach > 1:
            v = v + ccr[reach - 2, q].astype(F32)
        spst[s] = v.astype(BF)

        @pl.when(s != me)
        def _():
            sp_copy(s, me).start()

    for f in range(2):
        core_copy(y, f).wait_recv()
        up_copy(reach - 1, f).wait_recv()
        if reach > 1:
            down_copy(reach - 2, f).wait_recv()
        each(f, spread)
    spr[me] = spst[me]

    def wait_sp(i):
        sp_copy(lax.rem(me + i, ns), lax.rem(me + i, ns)).wait_recv()

    loop(1, ns, wait_sp)
    finr[core, y] = jnp.sum(spr[...].astype(F32), axis=0)

    def ag_copy(d, s):
        slot = finr.at[lax.rem(s, 2), s // 2]
        return remote(slot, slot, ag_s.at[d], ag_r.at[s], {"dp": d})

    def send_ag(i):
        ag_copy(lax.rem(dp + i, ndp), dp).start()

    loop(1, ndp, send_ag)

    def wait_back(i):
        back_copy(lax.rem(me + i, ns), lax.rem(me + i, ns)).wait_recv()

    loop(1, ns, wait_back)

    def pull(k):
        tile = owners[k]
        g = ret[jnp.minimum(tile // tpd, ns - 1)].astype(F32)
        g = jnp.where(tile < tpd * ns, g, 0.0)
        n, scale = normed(clips[k].astype(F32))
        v = n * gam
        sig = 1.0 / (1.0 + jnp.exp(-v))
        dn = g * sig * (1.0 + v * (1.0 - sig)) * gam
        gin[k] = (scale * (dn - n * jnp.mean(dn * n, axis=-1, keepdims=True))).astype(BF)

    loop(0, clips.shape[0], pull, 4)

    def wait_ag(i):
        d = lax.rem(dp + i, ndp)
        ag_copy(d, d).wait_recv()

    loop(1, ndp, wait_ag)
    for h in range(2):
        for k in range(ny):
            fin[h, k * rc : (k + 1) * rc, :] = finr[h, k]

    def done_space(i):
        d = lax.rem(me + i, ns)
        tile_copy(d, me).wait_send()
        back_copy(d, me).wait_send()
        sp_copy(d, me).wait_send()

    loop(1, ns, done_space)

    def done_dp(i):
        ag_copy(lax.rem(dp + i, ndp), dp).wait_send()

    loop(1, ndp, done_dp)

    for i in range(1, nx):
        id_x(lax.rem(xme + i, nx), xme).wait_send()
    for i in range(1, nz):
        id_z(lax.rem(zme + i, nz), zme).wait_send()

    def done_core(k):
        for f in range(2):
            core_copy(k, f).wait_send()

    loop(0, ny, done_core)
    for f in range(2):
        for i in range(reach):
            up_copy(i, f).wait_send()
        for i in range(reach - 1):
            down_copy(i, f).wait_send()

    @pl.when(me < ns - 1)
    def _():
        cot_copy.wait_send()

    @pl.when(me > 0)
    def _():
        row_copy.wait_send()


def flows(ns, wrows):
    kinds = [[], []]
    for s in range(ns):
        taps = range(s * wrows // 128, (s * wrows + wrows - 1) // 128 + 1)
        kinds[1 if any((tap % 9) // 3 == 2 for tap in taps) else 0].append(s)
    found = []
    q = 0
    for kind in kinds:
        ranges = []
        for s in kind:
            if ranges and ranges[-1][1] + ranges[-1][2] == s:
                ranges[-1] = (ranges[-1][0], q + 1, ranges[-1][2])
            else:
                ranges.append((q, q + 1, s - q))
            q += 1
        found.append(tuple(ranges))
    return tuple(found)


def local(clips, a_tile, gamma, weight, cotangent):
    ns = lax.axis_size("space")
    ny = lax.axis_size("dp") // 2
    me = lax.axis_index("space")
    frames, rows_in, tcols, chans = clips.shape[2:]
    half = cotangent.shape[3]
    tpd = half // 2
    cap = clips.shape[1]
    fj = frames * half
    trows = frames * rows_in * tcols
    wrows = weight.shape[0] // ns
    nx = 4
    rc = 16 * -(-(wrows + 12) // (16 * ny))
    pad = max(((s * wrows) // 16) * 16 + rc * ny for s in range(ns))
    vmem = pl.BlockSpec(memory_space=pltpu.VMEM)
    smem = pl.BlockSpec(memory_space=pltpu.SMEM)
    hbm = pl.BlockSpec(memory_space=pltpu.HBM)
    dma = pltpu.SemaphoreType.DMA
    tiles_shape = pltpu.VMEM((ns, trows, chans), BF)
    reach = ny // 2
    piece = (ns, rc, 128)
    out, gin, fin = pl.pallas_call(
        functools.partial(kernel, (ns, nx, ny, frames, half, wrows, rc, flows(ns, wrows))),
        out_shape=(
            jax.ShapeDtypeStruct((fj, 256), BF),
            jax.ShapeDtypeStruct((cap, trows, chans), BF),
            jax.ShapeDtypeStruct((2, rc * ny, 128), F32),
        ),
        in_specs=[smem, vmem, hbm, vmem, hbm, hbm],
        out_specs=(vmem, vmem, vmem),
        scratch_shapes=[
            pltpu.VMEM((cap, trows, chans), BF),
            pltpu.VMEM(weight.shape, BF),
            pltpu.VMEM((fj, 256), BF),
            pltpu.VMEM((fj, 256), BF),
            pltpu.VMEM((cap, trows, chans), BF),
            pltpu.VMEM((ns, 128), jnp.int32),
            pltpu.SMEM((ns, 128), jnp.int32),
            tiles_shape,
            tiles_shape,
            tiles_shape,
            tiles_shape,
            pltpu.VMEM((ns, 1, 128), jnp.int32),
            pltpu.VMEM((ns + 8, 128), jnp.int32),
            pltpu.SMEM((ns + 8, 128), jnp.int32),
            pltpu.VMEM((tpd, trows, chans), F32),
            pltpu.VMEM((tpd, trows, chans), BF),
            pltpu.VMEM((4, fj, chans), F32),
            pltpu.VMEM((4, fj, chans), F32),
            pltpu.VMEM((fj, 3 * chans), F32),
            pltpu.VMEM((tpd, trows, chans), F32),
            pltpu.VMEM((fj, 9 * chans), BF),
            pltpu.VMEM((2, pad, 128), F32),
            pltpu.VMEM((ny,) + piece, BF),
            pltpu.VMEM((ny,) + piece, BF),
            pltpu.VMEM((reach,) + piece, BF),
            pltpu.VMEM((reach,) + piece, BF),
            pltpu.VMEM((max(reach - 1, 1),) + piece, BF),
            pltpu.VMEM((max(reach - 1, 1),) + piece, BF),
            pltpu.VMEM(piece, BF),
            pltpu.VMEM(piece, BF),
            pltpu.VMEM((2, ny, rc, 128), F32),
            dma((5,)),
            dma((nx + ns // nx,)),
            dma((nx + ns // nx,)),
            dma((ns,)),
            dma((ns,)),
            dma((ns,)),
            dma((ns,)),
            dma((2,)),
            dma((2,)),
            dma((2, ny)),
            dma((2, ny)),
            dma((2, reach)),
            dma((2, reach)),
            dma((2, reach)),
            dma((2, reach)),
            dma((ns,)),
            dma((ns,)),
            dma((2 * ny,)),
            dma((2 * ny,)),
        ],
        compiler_params=pltpu.CompilerParams(
            collective_id=0, has_side_effects=True, vmem_limit_bytes=56 * 1024 * 1024
        ),
    )(
        a_tile[0],
        jnp.pad(a_tile, ((0, 0), (0, 128 - cap)), constant_values=tpd * ns),
        clips.reshape(cap, trows, chans),
        gamma.reshape(1, chans),
        weight,
        cotangent.reshape(fj, 256),
    )
    both = jnp.concatenate([fin[0], fin[1]], axis=1)
    first = me * wrows
    grad_weight = lax.dynamic_slice_in_dim(both, first - (first // 16) * 16, wrows, 0)
    return (
        out.reshape(1, frames, 1, half, 256),
        gin.reshape(clips.shape),
        grad_weight,
    )


def solution(mesh):
    return jax.shard_map(
        local,
        mesh=mesh,
        in_specs=(
            P("dp", "space", None, None, None, None),
            P("dp", "space"),
            P(),
            P(),
            P("dp", None, "space", None, None),
        ),
        out_specs=(
            P("dp", None, "space", None, None),
            P("dp", "space", None, None, None, None),
            P("space", None),
        ),
        check_vma=False,
    )
```

```python
import functools

import jax
import jax.numpy as jnp
from jax import lax
from jax.experimental import pallas as pl
from jax.experimental.pallas import tpu as pltpu
from jax.sharding import PartitionSpec as P

TPD = 16
BF = jnp.bfloat16
F32 = jnp.float32
NN = (((1,), (0,)), ((), ()))
NT = (((1,), (1,)), ((), ()))
TN = (((0,), (0,)), ((), ()))


def remote(src, dst, ssem, rsem, dev):
    return pltpu.make_async_remote_copy(
        src_ref=src,
        dst_ref=dst,
        send_sem=ssem,
        recv_sem=rsem,
        device_id=dev,
        device_id_type=pl.DeviceIdType.MESH,
    )


def loop(lo, hi, body, unroll=1):
    def step(i, carry):
        body(i)
        return carry

    lax.fori_loop(lo, hi, step, 0, unroll=unroll)


def normed(x):
    meansq = jnp.mean(x * x, axis=-1, keepdims=True)
    scale = lax.rsqrt(meansq + 1e-06)
    return x * scale, scale


def kernel(
    dims,
    owners,
    ids,
    clips_h,
    gamma,
    weight_h,
    cot_h,
    out,
    gin,
    fin,
    clips,
    weight,
    cot,
    cotprev,
    hid,
    slot_v,
    slot_s,
    stage,
    arr,
    stage2,
    ret,
    locr,
    map_v,
    map_s,
    tile32,
    tiles,
    planes,
    grads,
    gown,
    gtile32,
    xmat,
    gmat,
    cs,
    cr,
    cws,
    cwr,
    ccs,
    ccr,
    spst,
    spr,
    finr,
    in_sem,
    id_s,
    id_r,
    st_s,
    st_r,
    rt_s,
    rt_r,
    hop_s,
    hop_r,
    core_s,
    core_r,
    cw_s,
    cw_r,
    cc_s,
    cc_r,
    sp_s,
    sp_r,
    ag_s,
    ag_r,
):
    ns, nx, ny, frames, half, wrows, rc, flows = dims
    spans = [(f[0][0], f[-1][1]) for f in flows]
    ndp = 2 * ny
    chans = 128
    tpd = half // 2
    me = lax.axis_index("space")
    dp = lax.axis_index("dp")
    y = dp // 2
    core = lax.rem(dp, 2)
    fj = frames * half

    def begin(k):
        return ((k * wrows) // 16) * 16

    loads = [
        pltpu.make_async_copy(clips_h, clips, in_sem.at[0]),
        pltpu.make_async_copy(cot_h, cot, in_sem.at[1]),
        pltpu.make_async_copy(weight_h, weight, in_sem.at[2]),
    ]
    for load in loads:
        load.start()
    barrier = pltpu.get_barrier_semaphore()

    def greet_space(i):
        pl.semaphore_signal(
            barrier,
            inc=1,
            device_id={"space": lax.rem(me + i, ns)},
            device_id_type=pl.DeviceIdType.MESH,
        )

    def greet_dp(i):
        pl.semaphore_signal(
            barrier,
            inc=1,
            device_id={"dp": lax.rem(dp + i, ndp)},
            device_id_type=pl.DeviceIdType.MESH,
        )

    loop(1, ns, greet_space)
    loop(1, ndp, greet_dp)

    @pl.when(me == 0)
    def _():
        cotprev[...] = jnp.zeros(cotprev.shape, BF)

    @pl.when(me == ns - 1)
    def _():
        xmat[:, 6 * chans : 8 * chans] = jnp.zeros((fj, 2 * chans), BF)

    gmat[:, 27 * chans :, :] = jnp.zeros((2, gmat.shape[1] - 27 * chans, 128), F32)
    shape = (ns, 128)
    none = jnp.full((1, 128 - ids.shape[1]), tpd * ns, jnp.int32)
    id_row = jnp.concatenate([ids[...], none], axis=1)
    own_ids = jnp.broadcast_to(id_row, shape)
    first_id = lax.broadcasted_iota(jnp.int32, shape, 0) * tpd
    match = (own_ids >= first_id) & (own_ids < first_id + tpd)
    slots = lax.broadcasted_iota(jnp.int32, shape, 1)
    slot_of = jnp.max(jnp.where(match, slots, 0), axis=1, keepdims=True)
    slot_of = jnp.minimum(slot_of, clips.shape[0] - 1)
    slot_v[...] = jnp.broadcast_to(slot_of, (ns, 128))
    locr[me] = id_row
    slot_copy = pltpu.make_async_copy(slot_v, slot_s, in_sem.at[4])
    slot_copy.start()

    gam = gamma[...]
    loads[0].wait()

    def hide(k):
        n, _ = normed(clips[k].astype(F32))
        v = n * gam
        hid[k] = (v / (1.0 + jnp.exp(-v))).astype(BF)

    loop(0, clips.shape[0], hide, 4)
    slot_copy.wait()

    def set_out(d):
        stage[d] = hid[slot_s[d, 0]]

    loop(0, ns, set_out, 4)
    arr[me] = stage[me]
    loads[1].wait()
    pl.semaphore_wait(barrier, ns - 1 + ndp - 1)

    zme = me // nx
    xme = lax.rem(me, nx)
    nz = ns // nx

    def id_x(d, s):
        return remote(
            locr.at[zme * nx + s], locr.at[zme * nx + s], id_s.at[d], id_r.at[s],
            {"space": zme * nx + d},
        )

    def id_z(d, s):
        rows = locr.at[pl.ds(s * nx, nx)]
        return remote(
            rows, rows, id_s.at[nx + d], id_r.at[nx + s], {"space": d * nx + xme}
        )

    def tile_copy(d, s):
        return remote(stage.at[d], arr.at[s], st_s.at[d], st_r.at[s], {"space": d})

    for i in range(1, nx):
        id_x(lax.rem(xme + i, nx), xme).start()

    above = lax.rem(me + ns - 1, ns)
    under = lax.rem(me + 1, ns)
    cot_copy = remote(cot, cotprev, hop_s.at[0], hop_r.at[0], {"space": under})
    row_copy = remote(
        xmat.at[:, 0 : 2 * chans],
        xmat.at[:, 6 * chans : 8 * chans],
        hop_s.at[1],
        hop_r.at[1],
        {"space": above},
    )

    def send_tile(i):
        tile_copy(lax.rem(me + i, ns), me).start()

    loop(1, ns, send_tile)

    @pl.when(me < ns - 1)
    def _():
        cot_copy.start()

    for i in range(1, nx):
        d = lax.rem(xme + i, nx)
        id_x(d, d).wait_recv()
    for i in range(1, nz):
        id_z(lax.rem(zme + i, nz), zme).start()

    loads[2].wait()
    colrow = lax.rem(lax.broadcasted_iota(jnp.int32, (fj, chans), 0), half)

    def wpart(a, b):
        return weight[pl.ds((a * 9 + b * 3) * chans, 3 * chans), :]

    def back(source, b):
        total = lax.dot_general(source[...], wpart(2, b), NT, preferred_element_type=F32)
        for a in (1, 0):
            skip = (2 - a) * half
            part = lax.dot_general(
                source[skip:, :], wpart(a, b), NT, preferred_element_type=F32
            )
            total = total + jnp.concatenate(
                [part, jnp.zeros((skip, 3 * chans), F32)], axis=0
            )
        return total

    def put_planes(total, b):
        moved = pltpu.roll(total[:, 2 * chans :], 1, 0)
        moved = jnp.where(colrow == 0, 0.0, moved)
        grads[2 * b] = total[:, :chans] + moved
        grads[2 * b + 1] = total[:, chans : 2 * chans]

    put_planes(back(cot, 1), 1)
    upper = back(cot, 0)
    gown[...] = upper

    for i in range(1, nz):
        d = lax.rem(zme + i, nz)
        id_z(d, d).wait_recv()
    every = locr[:, 0, :]
    low = me * tpd
    in_row = (every >= low) & (every < low + tpd)
    got = jnp.broadcast_to(
        jnp.max(jnp.where(in_row, every - low, -1), axis=1, keepdims=True), (ns, 128)
    )
    lane = lax.broadcasted_iota(jnp.int32, (ns, 128), 1)
    who = lax.broadcasted_iota(jnp.int32, (ns, 128), 0)
    src_of = jnp.max(jnp.where(got == lane, who, 0), axis=0, keepdims=True)
    map_v[0:ns, :] = got
    map_v[ns : ns + 8, :] = jnp.broadcast_to(src_of, (8, 128))
    to_scalar = pltpu.make_async_copy(map_v, map_s, in_sem.at[3])
    to_scalar.start()
    to_scalar.wait()

    def wait_tile(i):
        tile_copy(lax.rem(me + i, ns), lax.rem(me + i, ns)).wait_recv()

    loop(1, ns, wait_tile)

    def lay_tile(t):
        tile32[t] = arr[map_s[ns, t]].astype(F32)
        for b in range(2):
            for par in range(2):
                for jj in range(2):
                    planes[2 * b + par, pl.ds(2 * t + jj, frames, stride=half), :] = tile32[
                        t, pl.ds(b * 4 + jj * 2 + par, frames, stride=8), :
                    ]

    loop(0, tpd, lay_tile, 2)

    def next_col(even):
        return jnp.where(colrow == half - 1, 0.0, pltpu.roll(even, fj - 1, 0)).astype(BF)

    def put_rows(b):
        even = planes[2 * b]
        xmat[:, (3 * b) * chans : (3 * b + 1) * chans] = even.astype(BF)
        xmat[:, (3 * b + 1) * chans : (3 * b + 2) * chans] = planes[2 * b + 1].astype(BF)
        xmat[:, (3 * b + 2) * chans : (3 * b + 3) * chans] = next_col(even)

    put_rows(0)

    @pl.when(me > 0)
    def _():
        row_copy.start()

    put_rows(1)

    def weight_grad(b):
        for a in range(3):
            count = fj - (2 - a) * half
            part = lax.dot_general(
                xmat[0:count, 3 * b * chans : 3 * (b + 1) * chans],
                cot[fj - count :, :],
                TN,
                preferred_element_type=F32,
            )
            row = (9 * a + 3 * b) * chans
            gmat[0, row : row + 3 * chans, :] = part[:, :128]
            gmat[1, row : row + 3 * chans, :] = part[:, 128:]

    other = {"dp": 2 * y + 1 - core}

    def core_copy(k, f):
        lo, hi = spans[f]
        return remote(
            cs.at[k, lo:hi], cr.at[k, lo:hi], core_s.at[f, k], core_r.at[f, k], other
        )

    ups = (ny // 2, ny - 1 - ny // 2)
    downs = (ups[1], ups[0])

    def each(f, body):
        for lo, hi, shift in flows[f]:
            loop(lo, hi, lambda q, shift=shift: body(q, q + shift))

    def send_core(f):
        def pack(q, s):
            row = pl.multiple_of(begin(s), 16)
            window = gmat[1 - core, pl.ds(row, rc * ny), :].astype(BF)
            cs[:, q] = window.reshape(ny, rc, 128)

        each(f, pack)
        for i in range(max(ups[f], downs[f])):
            if i < ups[f]:
                core_copy(lax.rem(y + ups[f] - i, ny), f).start()
            if i < downs[f]:
                core_copy(lax.rem(y + ny - downs[f] + i, ny), f).start()
        core_copy(y, f).start()

    def mine(k, q, s):
        row = pl.multiple_of(begin(s) + rc * k, 16)
        return gmat[core, pl.ds(row, rc), :] + cr[k, q].astype(F32)

    up = {"dp": 2 * lax.rem(y + 1, ny) + core}
    down = {"dp": 2 * lax.rem(y + ny - 1, ny) + core}

    def up_copy(i, f):
        lo, hi = spans[f]
        return remote(cws.at[i, lo:hi], cwr.at[i, lo:hi], cw_s.at[f, i], cw_r.at[f, i], up)

    def down_copy(i, f):
        lo, hi = spans[f]
        return remote(ccs.at[i, lo:hi], ccr.at[i, lo:hi], cc_s.at[f, i], cc_r.at[f, i], down)

    def hop(k, i, f, send, into, out_of):
        core_copy(k, f).wait_recv()
        if i > 0:
            send(i - 1, f).wait_recv()

        def add(q, s):
            v = mine(k, q, s)
            if i > 0:
                v = v + out_of[i - 1, q].astype(F32)
            into[i, q] = v.astype(BF)

        each(f, add)
        send(i, f).start()

    def chain(f, i):
        if i < ups[f]:
            hop(lax.rem(y + ups[f] - i, ny), i, f, up_copy, cws, cwr)
        if i < downs[f]:
            hop(lax.rem(y + ny - downs[f] + i, ny), i, f, down_copy, ccs, ccr)

    weight_grad(1)
    weight_grad(0)
    send_core(0)

    @pl.when(me > 0)
    def _():
        cot_copy.wait_recv()

    put_planes(gown[...] + back(cotprev, 2), 0)

    def cut_tile(t):
        for b in range(2):
            for par in range(2):
                for jj in range(2):
                    gtile32[t, pl.ds(b * 4 + jj * 2 + par, frames, stride=8), :] = grads[
                        2 * b + par, pl.ds(2 * t + jj, frames, stride=half), :
                    ]
        tiles[t] = gtile32[t].astype(BF)

    loop(0, tpd, cut_tile, 2)

    def back_copy(d, s):
        return remote(stage2.at[d], ret.at[s], rt_s.at[d], rt_r.at[s], {"space": d})

    def send_back(i):
        d = lax.rem(me + i, ns)
        stage2[d] = tiles[jnp.maximum(map_s[d, 0], 0)]
        back_copy(d, me).start()

    loop(1, ns, send_back)
    ret[me] = tiles[jnp.maximum(map_s[me, 0], 0)]

    chain(0, 0)

    @pl.when(me < ns - 1)
    def _():
        row_copy.wait_recv()

    xmat[:, 8 * chans : 9 * chans] = next_col(
        xmat[:, 6 * chans : 7 * chans].astype(F32)
    )
    weight_grad(2)
    send_core(1)
    chain(0, 1)
    chain(1, 0)

    total = lax.dot_general(xmat[...], weight[18 * chans :, :], NN, preferred_element_type=F32)
    for a in (1, 0):
        skip = (2 - a) * half
        part = lax.dot_general(
            xmat[0 : fj - skip, :],
            weight[9 * a * chans : 9 * (a + 1) * chans, :],
            NN,
            preferred_element_type=F32,
        )
        total = total + jnp.concatenate([jnp.zeros((skip, 256), F32), part], axis=0)
    out[...] = total.astype(BF)


    for i in range(2, max(ups)):
        chain(0, i)
        chain(1, i - 1)

    def sp_copy(d, s):
        return remote(spst.at[d], spr.at[s], sp_s.at[d], sp_r.at[s], {"space": d})

    def spread(f):
        core_copy(y, f).wait_recv()
        for send, steps in ((up_copy, ups), (down_copy, downs)):
            if steps[f] > 0:
                send(steps[f] - 1, f).wait_recv()

        def part(q, s):
            v = mine(y, q, s)
            for landed, steps in ((cwr, ups), (ccr, downs)):
                if steps[f] > 0:
                    v = v + landed[steps[f] - 1, q].astype(F32)
            spst[s] = v.astype(BF)

            @pl.when(s != me)
            def _():
                sp_copy(s, me).start()

        each(f, part)

    spread(0)
    chain(1, max(ups) - 1)
    spread(1)
    spr[me] = spst[me]

    def wait_sp(i):
        sp_copy(lax.rem(me + i, ns), lax.rem(me + i, ns)).wait_recv()

    loop(1, ns, wait_sp)
    finr[core, y] = jnp.sum(spr[...].astype(F32), axis=0)

    def ag_copy(d, s):
        slot = finr.at[lax.rem(s, 2), s // 2]
        return remote(slot, slot, ag_s.at[d], ag_r.at[s], {"dp": d})

    def send_ag(i):
        ag_copy(lax.rem(dp + i, ndp), dp).start()

    loop(1, ndp, send_ag)

    def wait_back(i):
        back_copy(lax.rem(me + i, ns), lax.rem(me + i, ns)).wait_recv()

    loop(1, ns, wait_back)

    def pull(k):
        tile = owners[k]
        g = ret[jnp.minimum(tile // tpd, ns - 1)].astype(F32)
        g = jnp.where(tile < tpd * ns, g, 0.0)
        n, scale = normed(clips[k].astype(F32))
        v = n * gam
        sig = 1.0 / (1.0 + jnp.exp(-v))
        dn = g * sig * (1.0 + v * (1.0 - sig)) * gam
        gin[k] = (scale * (dn - n * jnp.mean(dn * n, axis=-1, keepdims=True))).astype(BF)

    loop(0, clips.shape[0], pull, 4)

    def wait_ag(i):
        d = lax.rem(dp + i, ndp)
        ag_copy(d, d).wait_recv()

    loop(1, ndp, wait_ag)
    for off in range(0, 16, 4):

        @pl.when(me * wrows - begin(me) == off)
        def _(off=off):
            for h in range(2):
                window = finr[h].reshape(ny * rc, 128)
                fin[:, h * 128 : (h + 1) * 128] = window[off : off + wrows]

    def done_space(i):
        d = lax.rem(me + i, ns)
        tile_copy(d, me).wait_send()
        back_copy(d, me).wait_send()
        sp_copy(d, me).wait_send()

    loop(1, ns, done_space)

    def done_dp(i):
        ag_copy(lax.rem(dp + i, ndp), dp).wait_send()

    loop(1, ndp, done_dp)

    for i in range(1, nx):
        id_x(lax.rem(xme + i, nx), xme).wait_send()
    for i in range(1, nz):
        id_z(lax.rem(zme + i, nz), zme).wait_send()

    def done_core(k):
        for f in range(2):
            core_copy(k, f).wait_send()

    loop(0, ny, done_core)
    for f in range(2):
        for i in range(ups[f]):
            up_copy(i, f).wait_send()
        for i in range(downs[f]):
            down_copy(i, f).wait_send()

    @pl.when(me < ns - 1)
    def _():
        cot_copy.wait_send()

    @pl.when(me > 0)
    def _():
        row_copy.wait_send()


def pin(x):
    return pltpu.with_memory_space_constraint(x, pltpu.HBM)


def flows(ns, wrows):
    kinds = [[], []]
    for s in range(ns):
        taps = range(s * wrows // 128, (s * wrows + wrows - 1) // 128 + 1)
        kinds[1 if any((tap % 9) // 3 == 2 for tap in taps) else 0].append(s)
    found = []
    q = 0
    for kind in kinds:
        ranges = []
        for s in kind:
            if ranges and ranges[-1][1] + ranges[-1][2] == s:
                ranges[-1] = (ranges[-1][0], q + 1, ranges[-1][2])
            else:
                ranges.append((q, q + 1, s - q))
            q += 1
        found.append(tuple(ranges))
    return tuple(found)


def local(clips, a_tile, gamma, weight, cotangent):
    ns = lax.axis_size("space")
    ny = lax.axis_size("dp") // 2
    frames, rows_in, tcols, chans = clips.shape[2:]
    half = cotangent.shape[3]
    tpd = half // 2
    cap = clips.shape[1]
    fj = frames * half
    trows = frames * rows_in * tcols
    wrows = weight.shape[0] // ns
    nx = 4
    rc = 16 * -(-(wrows + 12) // (16 * ny))
    pad = max(((s * wrows) // 16) * 16 + rc * ny for s in range(ns))
    vmem = pl.BlockSpec(memory_space=pltpu.VMEM)
    smem = pl.BlockSpec(memory_space=pltpu.SMEM)
    hbm = pl.BlockSpec(memory_space=pltpu.HBM)
    dma = pltpu.SemaphoreType.DMA
    tiles_shape = pltpu.VMEM((ns, trows, chans), BF)
    reach = ny // 2
    piece = (ns, rc, 128)
    out, gin, fin = pl.pallas_call(
        functools.partial(kernel, (ns, nx, ny, frames, half, wrows, rc, flows(ns, wrows))),
        out_shape=(
            jax.ShapeDtypeStruct((fj, 256), BF),
            jax.ShapeDtypeStruct((cap, trows, chans), BF),
            jax.ShapeDtypeStruct((wrows, 256), F32),
        ),
        in_specs=[smem, vmem, hbm, vmem, hbm, hbm],
        out_specs=(vmem, vmem, vmem),
        scratch_shapes=[
            pltpu.VMEM((cap, trows, chans), BF),
            pltpu.VMEM(weight.shape, BF),
            pltpu.VMEM((fj, 256), BF),
            pltpu.VMEM((fj, 256), BF),
            pltpu.VMEM((cap, trows, chans), BF),
            pltpu.VMEM((ns, 128), jnp.int32),
            pltpu.SMEM((ns, 128), jnp.int32),
            tiles_shape,
            tiles_shape,
            tiles_shape,
            tiles_shape,
            pltpu.VMEM((ns, 1, 128), jnp.int32),
            pltpu.VMEM((ns + 8, 128), jnp.int32),
            pltpu.SMEM((ns + 8, 128), jnp.int32),
            pltpu.VMEM((tpd, trows, chans), F32),
            pltpu.VMEM((tpd, trows, chans), BF),
            pltpu.VMEM((4, fj, chans), F32),
            pltpu.VMEM((4, fj, chans), F32),
            pltpu.VMEM((fj, 3 * chans), F32),
            pltpu.VMEM((tpd, trows, chans), F32),
            pltpu.VMEM((fj, 9 * chans), BF),
            pltpu.VMEM((2, pad, 128), F32),
            pltpu.VMEM((ny,) + piece, BF),
            pltpu.VMEM((ny,) + piece, BF),
            pltpu.VMEM((reach,) + piece, BF),
            pltpu.VMEM((reach,) + piece, BF),
            pltpu.VMEM((reach,) + piece, BF),
            pltpu.VMEM((reach,) + piece, BF),
            pltpu.VMEM(piece, BF),
            pltpu.VMEM(piece, BF),
            pltpu.VMEM((2, ny, rc, 128), F32),
            dma((5,)),
            dma((nx + ns // nx,)),
            dma((nx + ns // nx,)),
            dma((ns,)),
            dma((ns,)),
            dma((ns,)),
            dma((ns,)),
            dma((2,)),
            dma((2,)),
            dma((2, ny)),
            dma((2, ny)),
            dma((2, reach)),
            dma((2, reach)),
            dma((2, reach)),
            dma((2, reach)),
            dma((ns,)),
            dma((ns,)),
            dma((2 * ny,)),
            dma((2 * ny,)),
        ],
        compiler_params=pltpu.CompilerParams(
            collective_id=0, has_side_effects=True, vmem_limit_bytes=48 * 1024 * 1024
        ),
    )(
        pin(a_tile[0]),
        pin(a_tile),
        pin(clips.reshape(cap, trows, chans)),
        pin(gamma.reshape(1, chans)),
        pin(weight),
        pin(cotangent.reshape(fj, 256)),
    )
    return (
        out.reshape(1, frames, 1, half, 256),
        gin.reshape(clips.shape),
        fin,
    )


def solution(mesh):
    return jax.shard_map(
        local,
        mesh=mesh,
        in_specs=(
            P("dp", "space", None, None, None, None),
            P("dp", "space"),
            P(),
            P(),
            P("dp", None, "space", None, None),
        ),
        out_specs=(
            P("dp", None, "space", None, None),
            P("dp", "space", None, None, None, None),
            P("space", None),
        ),
        check_vma=False,
    )
```

```python
import functools

import jax
import jax.numpy as jnp
from jax import lax
from jax.experimental import pallas as pl
from jax.experimental.pallas import tpu as pltpu
from jax.sharding import PartitionSpec as P

TPD = 16
BF = jnp.bfloat16
F32 = jnp.float32
NN = (((1,), (0,)), ((), ()))
NT = (((1,), (1,)), ((), ()))
TN = (((0,), (0,)), ((), ()))


def remote(src, dst, ssem, rsem, dev):
    return pltpu.make_async_remote_copy(
        src_ref=src,
        dst_ref=dst,
        send_sem=ssem,
        recv_sem=rsem,
        device_id=dev,
        device_id_type=pl.DeviceIdType.MESH,
    )


def loop(lo, hi, body, unroll=1):
    def step(i, carry):
        body(i)
        return carry

    lax.fori_loop(lo, hi, step, 0, unroll=unroll)


def normed(x):
    meansq = jnp.mean(x * x, axis=-1, keepdims=True)
    scale = lax.rsqrt(meansq + 1e-06)
    return x * scale, scale


def kernel(
    dims,
    owners,
    ids,
    clips_h,
    gamma,
    weight_h,
    cot_h,
    out,
    gin,
    fin,
    clips,
    weight,
    cot,
    cotprev,
    hid,
    slot_v,
    slot_s,
    stage,
    arr,
    stage2,
    ret,
    locr,
    map_v,
    map_s,
    tile32,
    tiles,
    planes,
    grads,
    gown,
    gtile32,
    xmat,
    gmat,
    cs,
    cr,
    cws,
    cwr,
    ccs,
    ccr,
    spst,
    spr,
    finr,
    in_sem,
    id_s,
    id_r,
    st_s,
    st_r,
    rt_s,
    rt_r,
    hop_s,
    hop_r,
    core_s,
    core_r,
    cw_s,
    cw_r,
    cc_s,
    cc_r,
    sp_s,
    sp_r,
    ag_s,
    ag_r,
    late_sem,
):
    ns, nx, ny, frames, half, wrows, rc, flows = dims
    spans = [(f[0][0], f[-1][1]) for f in flows]
    ndp = 2 * ny
    chans = 128
    tpd = half // 2
    me = lax.axis_index("space")
    dp = lax.axis_index("dp")
    y = dp // 2
    core = lax.rem(dp, 2)
    fj = frames * half

    def begin(k):
        return ((k * wrows) // 16) * 16

    loads = [
        pltpu.make_async_copy(clips_h, clips, in_sem.at[0]),
        pltpu.make_async_copy(cot_h, cot, in_sem.at[1]),
        pltpu.make_async_copy(weight_h, weight, in_sem.at[2]),
    ]
    for load in loads:
        load.start()
    barrier = pltpu.get_barrier_semaphore()

    def greet_space(i):
        pl.semaphore_signal(
            barrier,
            inc=1,
            device_id={"space": lax.rem(me + i, ns)},
            device_id_type=pl.DeviceIdType.MESH,
        )

    def greet_dp(sem, j, other_core):
        pl.semaphore_signal(
            sem,
            inc=1,
            device_id={"dp": 2 * j + other_core},
            device_id_type=pl.DeviceIdType.MESH,
        )

    loop(1, ny, lambda i: greet_dp(barrier, lax.rem(y + i, ny), core))

    @pl.when(core == 1)
    def _():
        loop(0, ny, lambda j: greet_dp(barrier, j, 0))

    loop(1, ns, greet_space)

    @pl.when(me == 0)
    def _():
        cotprev[...] = jnp.zeros(cotprev.shape, BF)

    @pl.when(me == ns - 1)
    def _():
        xmat[:, 6 * chans : 8 * chans] = jnp.zeros((fj, 2 * chans), BF)

    gmat[:, 27 * chans :, :] = jnp.zeros((2, gmat.shape[1] - 27 * chans, 128), F32)
    shape = (ns, 128)
    none = jnp.full((1, 128 - ids.shape[1]), tpd * ns, jnp.int32)
    id_row = jnp.concatenate([ids[...], none], axis=1)
    own_ids = jnp.broadcast_to(id_row, shape)
    first_id = lax.broadcasted_iota(jnp.int32, shape, 0) * tpd
    match = (own_ids >= first_id) & (own_ids < first_id + tpd)
    slots = lax.broadcasted_iota(jnp.int32, shape, 1)
    slot_of = jnp.max(jnp.where(match, slots, 0), axis=1, keepdims=True)
    slot_of = jnp.minimum(slot_of, clips.shape[0] - 1)
    slot_v[...] = jnp.broadcast_to(slot_of, (ns, 128))
    locr[me] = id_row
    slot_copy = pltpu.make_async_copy(slot_v, slot_s, in_sem.at[4])
    slot_copy.start()

    gam = gamma[...]
    loads[0].wait()

    gam_half = gam * 0.5

    def hide(k):
        x = clips[k].astype(F32)
        h = x * lax.rsqrt(jnp.mean(x * x, axis=-1, keepdims=True) + 1e-06) * gam_half
        hid[k] = (h + h * jnp.tanh(h)).astype(BF)

    loop(0, clips.shape[0], hide, 4)
    slot_copy.wait()

    def set_out(d):
        stage[d] = hid[slot_s[d, 0]]

    loop(0, ns, set_out, 4)
    arr[me] = stage[me]
    loads[1].wait()
    pl.semaphore_wait(barrier, ns - 1 + ny - 1 + ny * (1 - core))

    zme = me // nx
    xme = lax.rem(me, nx)
    nz = ns // nx

    def id_x(d, s):
        return remote(
            locr.at[zme * nx + s], locr.at[zme * nx + s], id_s.at[d], id_r.at[s],
            {"space": zme * nx + d},
        )

    def id_z(d, s):
        rows = locr.at[pl.ds(s * nx, nx)]
        return remote(
            rows, rows, id_s.at[nx + d], id_r.at[nx + s], {"space": d * nx + xme}
        )

    def tile_copy(d, s):
        return remote(stage.at[d], arr.at[s], st_s.at[d], st_r.at[s], {"space": d})

    for i in range(1, nx):
        id_x(lax.rem(xme + i, nx), xme).start()

    above = lax.rem(me + ns - 1, ns)
    under = lax.rem(me + 1, ns)
    cot_copy = remote(cot, cotprev, hop_s.at[0], hop_r.at[0], {"space": under})
    row_copy = remote(
        xmat.at[:, 0 : 2 * chans],
        xmat.at[:, 6 * chans : 8 * chans],
        hop_s.at[1],
        hop_r.at[1],
        {"space": above},
    )

    def send_tile(i):
        tile_copy(lax.rem(me + i, ns), me).start()

    loop(1, ns, send_tile)

    @pl.when(me < ns - 1)
    def _():
        cot_copy.start()

    @pl.when(core == 0)
    def _():
        loop(0, ny, lambda j: greet_dp(late_sem, j, 1))

    for i in range(1, nx):
        d = lax.rem(xme + i, nx)
        id_x(d, d).wait_recv()
    for i in range(1, nz):
        id_z(lax.rem(zme + i, nz), zme).start()

    loads[2].wait()
    colrow = lax.rem(lax.broadcasted_iota(jnp.int32, (fj, chans), 0), half)

    def wpart(a, b):
        return weight[pl.ds((a * 9 + b * 3) * chans, 3 * chans), :]

    def back(source, b):
        total = lax.dot_general(source[...], wpart(2, b), NT, preferred_element_type=F32)
        for a in (1, 0):
            skip = (2 - a) * half
            part = lax.dot_general(
                source[skip:, :], wpart(a, b), NT, preferred_element_type=F32
            )
            total = total + jnp.concatenate(
                [part, jnp.zeros((skip, 3 * chans), F32)], axis=0
            )
        return total

    def put_planes(total, b):
        moved = pltpu.roll(total[:, 2 * chans :], 1, 0)
        moved = jnp.where(colrow == 0, 0.0, moved)
        grads[2 * b] = total[:, :chans] + moved
        grads[2 * b + 1] = total[:, chans : 2 * chans]

    put_planes(back(cot, 1), 1)
    upper = back(cot, 0)
    gown[...] = upper

    for i in range(1, nz):
        d = lax.rem(zme + i, nz)
        id_z(d, d).wait_recv()
    every = locr[:, 0, :]
    low = me * tpd
    in_row = (every >= low) & (every < low + tpd)
    got = jnp.broadcast_to(
        jnp.max(jnp.where(in_row, every - low, -1), axis=1, keepdims=True), (ns, 128)
    )
    lane = lax.broadcasted_iota(jnp.int32, (ns, 128), 1)
    who = lax.broadcasted_iota(jnp.int32, (ns, 128), 0)
    src_of = jnp.max(jnp.where(got == lane, who, 0), axis=0, keepdims=True)
    map_v[0:ns, :] = got
    map_v[ns : ns + 8, :] = jnp.broadcast_to(src_of, (8, 128))
    to_scalar = pltpu.make_async_copy(map_v, map_s, in_sem.at[3])
    to_scalar.start()
    to_scalar.wait()

    def wait_tile(i):
        tile_copy(lax.rem(me + i, ns), lax.rem(me + i, ns)).wait_recv()

    loop(1, ns, wait_tile)

    def lay_tile(t):
        tile32[t] = arr[map_s[ns, t]].astype(F32)
        for b in range(2):
            for par in range(2):
                for jj in range(2):
                    planes[2 * b + par, pl.ds(2 * t + jj, frames, stride=half), :] = tile32[
                        t, pl.ds(b * 4 + jj * 2 + par, frames, stride=8), :
                    ]

    loop(0, tpd, lay_tile, 2)

    def next_col(even):
        return jnp.where(colrow == half - 1, 0.0, pltpu.roll(even, fj - 1, 0)).astype(BF)

    def put_rows(b):
        even = planes[2 * b]
        xmat[:, (3 * b) * chans : (3 * b + 1) * chans] = even.astype(BF)
        xmat[:, (3 * b + 1) * chans : (3 * b + 2) * chans] = planes[2 * b + 1].astype(BF)
        xmat[:, (3 * b + 2) * chans : (3 * b + 3) * chans] = next_col(even)

    put_rows(0)

    @pl.when(me > 0)
    def _():
        row_copy.start()

    put_rows(1)

    def weight_grad(b):
        for a in range(3):
            count = fj - (2 - a) * half
            part = lax.dot_general(
                xmat[0:count, 3 * b * chans : 3 * (b + 1) * chans],
                cot[fj - count :, :],
                TN,
                preferred_element_type=F32,
            )
            row = (9 * a + 3 * b) * chans
            gmat[0, row : row + 3 * chans, :] = part[:, :128]
            gmat[1, row : row + 3 * chans, :] = part[:, 128:]

    other = {"dp": 2 * y + 1 - core}

    def core_copy(k, f):
        lo, hi = spans[f]
        return remote(
            cs.at[k, lo:hi], cr.at[k, lo:hi], core_s.at[f, k], core_r.at[f, k], other
        )

    ups = (ny // 2, ny - 1 - ny // 2)
    downs = (ups[1], ups[0])

    def each(f, body):
        for lo, hi, shift in flows[f]:
            loop(lo, hi, lambda q, shift=shift: body(q, q + shift))

    def send_core(f):
        def pack(q, s):
            row = pl.multiple_of(begin(s), 16)
            window = gmat[1 - core, pl.ds(row, rc * ny), :].astype(BF)
            cs[:, q] = window.reshape(ny, rc, 128)

        each(f, pack)
        for i in range(max(ups[f], downs[f])):
            if i < ups[f]:
                core_copy(lax.rem(y + ups[f] - i, ny), f).start()
            if i < downs[f]:
                core_copy(lax.rem(y + ny - downs[f] + i, ny), f).start()
        core_copy(y, f).start()

    def mine(k, q, s):
        row = pl.multiple_of(begin(s) + rc * k, 16)
        return gmat[core, pl.ds(row, rc), :] + cr[k, q].astype(F32)

    up = {"dp": 2 * lax.rem(y + 1, ny) + core}
    down = {"dp": 2 * lax.rem(y + ny - 1, ny) + core}

    def up_copy(i, f):
        lo, hi = spans[f]
        return remote(cws.at[i, lo:hi], cwr.at[i, lo:hi], cw_s.at[f, i], cw_r.at[f, i], up)

    def down_copy(i, f):
        lo, hi = spans[f]
        return remote(ccs.at[i, lo:hi], ccr.at[i, lo:hi], cc_s.at[f, i], cc_r.at[f, i], down)

    def hop(k, i, f, send, into, out_of):
        core_copy(k, f).wait_recv()
        if i > 0:
            send(i - 1, f).wait_recv()

        def add(q, s):
            v = mine(k, q, s)
            if i > 0:
                v = v + out_of[i - 1, q].astype(F32)
            into[i, q] = v.astype(BF)

        each(f, add)
        send(i, f).start()

    def chain(f, i):
        if i < ups[f]:
            hop(lax.rem(y + ups[f] - i, ny), i, f, up_copy, cws, cwr)
        if i < downs[f]:
            hop(lax.rem(y + ny - downs[f] + i, ny), i, f, down_copy, ccs, ccr)

    weight_grad(1)
    weight_grad(0)

    @pl.when(core == 1)
    def _():
        pl.semaphore_wait(late_sem, ny)

    send_core(0)

    @pl.when(me > 0)
    def _():
        cot_copy.wait_recv()

    put_planes(gown[...] + back(cotprev, 2), 0)

    def cut_tile(t):
        for b in range(2):
            for par in range(2):
                for jj in range(2):
                    gtile32[t, pl.ds(b * 4 + jj * 2 + par, frames, stride=8), :] = grads[
                        2 * b + par, pl.ds(2 * t + jj, frames, stride=half), :
                    ]
        tiles[t] = gtile32[t].astype(BF)

    loop(0, tpd, cut_tile, 2)

    chain(0, 0)

    def back_copy(d, s):
        return remote(stage2.at[d], ret.at[s], rt_s.at[d], rt_r.at[s], {"space": d})

    def send_back(i):
        d = lax.rem(me + i, ns)
        stage2[d] = tiles[jnp.maximum(map_s[d, 0], 0)]
        back_copy(d, me).start()

    loop(1, ns, send_back)
    ret[me] = tiles[jnp.maximum(map_s[me, 0], 0)]

    @pl.when(me < ns - 1)
    def _():
        row_copy.wait_recv()

    xmat[:, 8 * chans : 9 * chans] = next_col(
        xmat[:, 6 * chans : 7 * chans].astype(F32)
    )
    weight_grad(2)
    send_core(1)
    chain(0, 1)
    chain(1, 0)

    total = lax.dot_general(xmat[...], weight[18 * chans :, :], NN, preferred_element_type=F32)
    for a in (1, 0):
        skip = (2 - a) * half
        part = lax.dot_general(
            xmat[0 : fj - skip, :],
            weight[9 * a * chans : 9 * (a + 1) * chans, :],
            NN,
            preferred_element_type=F32,
        )
        total = total + jnp.concatenate([jnp.zeros((skip, 256), F32), part], axis=0)
    out[...] = total.astype(BF)


    for i in range(2, max(ups)):
        chain(0, i)
        chain(1, i - 1)

    def sp_copy(d, s):
        return remote(spst.at[d], spr.at[s], sp_s.at[d], sp_r.at[s], {"space": d})

    def spread(f):
        core_copy(y, f).wait_recv()
        for send, steps in ((up_copy, ups), (down_copy, downs)):
            if steps[f] > 0:
                send(steps[f] - 1, f).wait_recv()

        def part(q, s):
            v = mine(y, q, s)
            for landed, steps in ((cwr, ups), (ccr, downs)):
                if steps[f] > 0:
                    v = v + landed[steps[f] - 1, q].astype(F32)
            spst[s] = v.astype(BF)

            @pl.when(s != me)
            def _():
                sp_copy(s, me).start()

        each(f, part)

    def done_tiles(i):
        tile_copy(lax.rem(me + i, ns), me).wait_send()

    loop(1, ns, done_tiles)
    for i in range(1, nx):
        id_x(lax.rem(xme + i, nx), xme).wait_send()
    for i in range(1, nz):
        id_z(lax.rem(zme + i, nz), zme).wait_send()

    @pl.when(me < ns - 1)
    def _():
        cot_copy.wait_send()

    @pl.when(me > 0)
    def _():
        row_copy.wait_send()

    spread(0)
    chain(1, max(ups) - 1)
    spread(1)
    spr[me] = spst[me]

    def done_core(k):
        for f in range(2):
            core_copy(k, f).wait_send()

    loop(0, ny, done_core)
    for f in range(2):
        for i in range(ups[f]):
            up_copy(i, f).wait_send()
        for i in range(downs[f]):
            down_copy(i, f).wait_send()

    def wait_back(i):
        back_copy(lax.rem(me + i, ns), lax.rem(me + i, ns)).wait_recv()
        back_copy(lax.rem(me + i, ns), me).wait_send()

    loop(1, ns, wait_back)

    def pull(k):
        tile = owners[k]
        g = ret[jnp.minimum(tile // tpd, ns - 1)].astype(F32)
        g = jnp.where(tile < tpd * ns, g, 0.0)
        n, scale = normed(clips[k].astype(F32))
        v = n * gam
        sig = 0.5 + 0.5 * jnp.tanh(0.5 * v)
        dn = g * sig * (1.0 + v * (1.0 - sig)) * gam
        gin[k] = (scale * (dn - n * jnp.mean(dn * n, axis=-1, keepdims=True))).astype(BF)

    middle = clips.shape[0] // 2
    loop(0, middle, pull, 4)

    def wait_sp(i):
        sp_copy(lax.rem(me + i, ns), lax.rem(me + i, ns)).wait_recv()

    loop(1, ns, wait_sp)
    finr[core, y] = jnp.sum(spr[...].astype(F32), axis=0)

    def ag_copy(d, s):
        slot = finr.at[lax.rem(s, 2), s // 2]
        return remote(slot, slot, ag_s.at[d], ag_r.at[s], {"dp": d})

    def send_ag(i):
        ag_copy(lax.rem(dp + i, ndp), dp).start()

    loop(1, ndp, send_ag)

    loop(middle, clips.shape[0], pull, 4)

    def done_sp(i):
        sp_copy(lax.rem(me + i, ns), me).wait_send()

    loop(1, ns, done_sp)

    def wait_ag(i):
        d = lax.rem(dp + i, ndp)
        ag_copy(d, d).wait_recv()

    loop(1, ndp, wait_ag)
    for off in range(0, 16, 4):

        @pl.when(me * wrows - begin(me) == off)
        def _(off=off):
            for h in range(2):
                window = finr[h].reshape(ny * rc, 128)
                fin[:, h * 128 : (h + 1) * 128] = window[off : off + wrows]

    def done_dp(i):
        ag_copy(lax.rem(dp + i, ndp), dp).wait_send()

    loop(1, ndp, done_dp)


def pin(x):
    return pltpu.with_memory_space_constraint(x, pltpu.HBM)


def flows(ns, wrows):
    kinds = [[], []]
    for s in range(ns):
        taps = range(s * wrows // 128, (s * wrows + wrows - 1) // 128 + 1)
        kinds[1 if any((tap % 9) // 3 == 2 for tap in taps) else 0].append(s)
    found = []
    q = 0
    for kind in kinds:
        ranges = []
        for s in kind:
            if ranges and ranges[-1][1] + ranges[-1][2] == s:
                ranges[-1] = (ranges[-1][0], q + 1, ranges[-1][2])
            else:
                ranges.append((q, q + 1, s - q))
            q += 1
        found.append(tuple(ranges))
    return tuple(found)


def local(clips, a_tile, gamma, weight, cotangent):
    ns = lax.axis_size("space")
    ny = lax.axis_size("dp") // 2
    frames, rows_in, tcols, chans = clips.shape[2:]
    half = cotangent.shape[3]
    tpd = half // 2
    cap = clips.shape[1]
    fj = frames * half
    trows = frames * rows_in * tcols
    wrows = weight.shape[0] // ns
    nx = 4
    rc = 16 * -(-(wrows + 12) // (16 * ny))
    pad = max(((s * wrows) // 16) * 16 + rc * ny for s in range(ns))
    vmem = pl.BlockSpec(memory_space=pltpu.VMEM)
    smem = pl.BlockSpec(memory_space=pltpu.SMEM)
    hbm = pl.BlockSpec(memory_space=pltpu.HBM)
    dma = pltpu.SemaphoreType.DMA
    tiles_shape = pltpu.VMEM((ns, trows, chans), BF)
    reach = ny // 2
    piece = (ns, rc, 128)
    out, gin, fin = pl.pallas_call(
        functools.partial(kernel, (ns, nx, ny, frames, half, wrows, rc, flows(ns, wrows))),
        out_shape=(
            jax.ShapeDtypeStruct((fj, 256), BF),
            jax.ShapeDtypeStruct((cap, trows, chans), BF),
            jax.ShapeDtypeStruct((wrows, 256), F32),
        ),
        in_specs=[smem, vmem, hbm, vmem, hbm, hbm],
        out_specs=(vmem, vmem, vmem),
        scratch_shapes=[
            pltpu.VMEM((cap, trows, chans), BF),
            pltpu.VMEM(weight.shape, BF),
            pltpu.VMEM((fj, 256), BF),
            pltpu.VMEM((fj, 256), BF),
            pltpu.VMEM((cap, trows, chans), BF),
            pltpu.VMEM((ns, 128), jnp.int32),
            pltpu.SMEM((ns, 128), jnp.int32),
            tiles_shape,
            tiles_shape,
            tiles_shape,
            tiles_shape,
            pltpu.VMEM((ns, 1, 128), jnp.int32),
            pltpu.VMEM((ns + 8, 128), jnp.int32),
            pltpu.SMEM((ns + 8, 128), jnp.int32),
            pltpu.VMEM((tpd, trows, chans), F32),
            pltpu.VMEM((tpd, trows, chans), BF),
            pltpu.VMEM((4, fj, chans), F32),
            pltpu.VMEM((4, fj, chans), F32),
            pltpu.VMEM((fj, 3 * chans), F32),
            pltpu.VMEM((tpd, trows, chans), F32),
            pltpu.VMEM((fj, 9 * chans), BF),
            pltpu.VMEM((2, pad, 128), F32),
            pltpu.VMEM((ny,) + piece, BF),
            pltpu.VMEM((ny,) + piece, BF),
            pltpu.VMEM((reach,) + piece, BF),
            pltpu.VMEM((reach,) + piece, BF),
            pltpu.VMEM((reach,) + piece, BF),
            pltpu.VMEM((reach,) + piece, BF),
            pltpu.VMEM(piece, BF),
            pltpu.VMEM(piece, BF),
            pltpu.VMEM((2, ny, rc, 128), F32),
            dma((5,)),
            dma((nx + ns // nx,)),
            dma((nx + ns // nx,)),
            dma((ns,)),
            dma((ns,)),
            dma((ns,)),
            dma((ns,)),
            dma((2,)),
            dma((2,)),
            dma((2, ny)),
            dma((2, ny)),
            dma((2, reach)),
            dma((2, reach)),
            dma((2, reach)),
            dma((2, reach)),
            dma((ns,)),
            dma((ns,)),
            dma((2 * ny,)),
            dma((2 * ny,)),
            pltpu.SemaphoreType.REGULAR,
        ],
        compiler_params=pltpu.CompilerParams(
            collective_id=0, has_side_effects=True, vmem_limit_bytes=48 * 1024 * 1024
        ),
    )(
        pin(a_tile[0]),
        pin(a_tile),
        pin(clips.reshape(cap, trows, chans)),
        pin(gamma.reshape(1, chans)),
        pin(weight),
        pin(cotangent.reshape(fj, 256)),
    )
    return (
        out.reshape(1, frames, 1, half, 256),
        gin.reshape(clips.shape),
        fin,
    )


def solution(mesh):
    return jax.shard_map(
        local,
        mesh=mesh,
        in_specs=(
            P("dp", "space", None, None, None, None),
            P("dp", "space"),
            P(),
            P(),
            P("dp", None, "space", None, None),
        ),
        out_specs=(
            P("dp", None, "space", None, None),
            P("dp", "space", None, None, None, None),
            P("space", None),
        ),
        check_vma=False,
    )
```

```python
import functools

import jax
import jax.numpy as jnp
from jax import lax
from jax.experimental import pallas as pl
from jax.experimental.pallas import tpu as pltpu
from jax.sharding import PartitionSpec as P

TPD = 16
BF = jnp.bfloat16
F32 = jnp.float32
NN = (((1,), (0,)), ((), ()))
NT = (((1,), (1,)), ((), ()))
TN = (((0,), (0,)), ((), ()))


def remote(src, dst, ssem, rsem, dev):
    return pltpu.make_async_remote_copy(
        src_ref=src,
        dst_ref=dst,
        send_sem=ssem,
        recv_sem=rsem,
        device_id=dev,
        device_id_type=pl.DeviceIdType.MESH,
    )


def loop(lo, hi, body, unroll=1):
    def step(i, carry):
        body(i)
        return carry

    lax.fori_loop(lo, hi, step, 0, unroll=unroll)


def normed(x):
    meansq = jnp.mean(x * x, axis=-1, keepdims=True)
    scale = lax.rsqrt(meansq + 1e-06)
    return x * scale, scale


def kernel(
    dims,
    owners,
    ids,
    clips_h,
    gamma,
    weight_h,
    cot_h,
    out,
    gin,
    fin,
    clips,
    weight,
    cot,
    cotprev,
    hid,
    slot_v,
    slot_s,
    stage,
    arr,
    stage2,
    ret,
    locr,
    map_v,
    map_s,
    tile32,
    tiles,
    planes,
    grads,
    gown,
    gtile32,
    xmat,
    gmat,
    cs,
    cr,
    cws,
    cwr,
    ccs,
    ccr,
    spst,
    spr,
    finr,
    in_sem,
    id_s,
    id_r,
    st_s,
    st_r,
    rt_s,
    rt_r,
    hop_s,
    hop_r,
    core_s,
    core_r,
    cw_s,
    cw_r,
    cc_s,
    cc_r,
    sp_s,
    sp_r,
    ag_s,
    ag_r,
    late_sem,
):
    ns, nx, ny, frames, half, wrows, rc, flows = dims
    spans = [(f[0][0], f[-1][1]) for f in flows]
    ndp = 2 * ny
    chans = 128
    tpd = half // 2
    me = lax.axis_index("space")
    dp = lax.axis_index("dp")
    y = dp // 2
    core = lax.rem(dp, 2)
    fj = frames * half

    def begin(k):
        return ((k * wrows) // 16) * 16

    loads = [
        pltpu.make_async_copy(clips_h, clips, in_sem.at[0]),
        pltpu.make_async_copy(cot_h, cot, in_sem.at[1]),
        pltpu.make_async_copy(weight_h, weight, in_sem.at[2]),
    ]
    for load in loads:
        load.start()
    barrier = pltpu.get_barrier_semaphore()

    def greet_space(i):
        pl.semaphore_signal(
            barrier,
            inc=1,
            device_id={"space": lax.rem(me + i, ns)},
            device_id_type=pl.DeviceIdType.MESH,
        )

    def greet_dp(sem, j, other_core):
        pl.semaphore_signal(
            sem,
            inc=1,
            device_id={"dp": 2 * j + other_core},
            device_id_type=pl.DeviceIdType.MESH,
        )

    loop(1, ny, lambda i: greet_dp(barrier, lax.rem(y + i, ny), core))

    @pl.when(core == 1)
    def _():
        loop(0, ny, lambda j: greet_dp(barrier, j, 0))

    loop(1, ns, greet_space)

    @pl.when(me == 0)
    def _():
        cotprev[...] = jnp.zeros(cotprev.shape, BF)

    @pl.when(me == ns - 1)
    def _():
        xmat[:, 6 * chans : 8 * chans] = jnp.zeros((fj, 2 * chans), BF)

    gmat[:, 27 * chans :, :] = jnp.zeros((2, gmat.shape[1] - 27 * chans, 128), F32)
    shape = (ns, 128)
    none = jnp.full((1, 128 - ids.shape[1]), tpd * ns, jnp.int32)
    id_row = jnp.concatenate([ids[...], none], axis=1)
    own_ids = jnp.broadcast_to(id_row, shape)
    first_id = lax.broadcasted_iota(jnp.int32, shape, 0) * tpd
    match = (own_ids >= first_id) & (own_ids < first_id + tpd)
    slots = lax.broadcasted_iota(jnp.int32, shape, 1)
    slot_of = jnp.max(jnp.where(match, slots, 0), axis=1, keepdims=True)
    slot_of = jnp.minimum(slot_of, clips.shape[0] - 1)
    slot_v[...] = jnp.broadcast_to(slot_of, (ns, 128))
    locr[me] = id_row
    slot_copy = pltpu.make_async_copy(slot_v, slot_s, in_sem.at[4])
    slot_copy.start()

    gam = gamma[...]
    loads[0].wait()

    gam_half = gam * 0.5

    def hide(k):
        x = clips[k].astype(F32)
        h = x * lax.rsqrt(jnp.mean(x * x, axis=-1, keepdims=True) + 1e-06) * gam_half
        hid[k] = (h + h * jnp.tanh(h)).astype(BF)

    loop(0, clips.shape[0], hide, 4)
    slot_copy.wait()

    def set_out(d):
        stage[d] = hid[slot_s[d, 0]]

    loop(0, ns, set_out, 4)
    arr[me] = stage[me]
    loads[1].wait()
    pl.semaphore_wait(barrier, ns - 1 + ny - 1 + ny * (1 - core))

    zme = me // nx
    xme = lax.rem(me, nx)
    nz = ns // nx

    def id_x(d, s):
        return remote(
            locr.at[zme * nx + s], locr.at[zme * nx + s], id_s.at[d], id_r.at[s],
            {"space": zme * nx + d},
        )

    def id_z(d, s):
        rows = locr.at[pl.ds(s * nx, nx)]
        return remote(
            rows, rows, id_s.at[nx + d], id_r.at[nx + s], {"space": d * nx + xme}
        )

    def tile_copy(d, s):
        return remote(stage.at[d], arr.at[s], st_s.at[d], st_r.at[s], {"space": d})

    for i in range(1, nx):
        id_x(lax.rem(xme + i, nx), xme).start()

    above = lax.rem(me + ns - 1, ns)
    under = lax.rem(me + 1, ns)
    cot_copy = remote(cot, cotprev, hop_s.at[0], hop_r.at[0], {"space": under})
    row_copy = remote(
        xmat.at[:, 0 : 2 * chans],
        xmat.at[:, 6 * chans : 8 * chans],
        hop_s.at[1],
        hop_r.at[1],
        {"space": above},
    )

    def send_tile(i):
        tile_copy(lax.rem(me + i, ns), me).start()

    loop(1, ns, send_tile)

    @pl.when(me < ns - 1)
    def _():
        cot_copy.start()

    @pl.when(core == 0)
    def _():
        loop(0, ny, lambda j: greet_dp(late_sem, j, 1))

    for i in range(1, nx):
        d = lax.rem(xme + i, nx)
        id_x(d, d).wait_recv()
    for i in range(1, nz):
        id_z(lax.rem(zme + i, nz), zme).start()

    loads[2].wait()
    colrow = lax.rem(lax.broadcasted_iota(jnp.int32, (fj, chans), 0), half)

    def wpart(a, b):
        return weight[pl.ds((a * 9 + b * 3) * chans, 3 * chans), :]

    def back(source, b):
        total = lax.dot_general(source[...], wpart(2, b), NT, preferred_element_type=F32)
        for a in (1, 0):
            skip = (2 - a) * half
            part = lax.dot_general(
                source[skip:, :], wpart(a, b), NT, preferred_element_type=F32
            )
            total = total + jnp.concatenate(
                [part, jnp.zeros((skip, 3 * chans), F32)], axis=0
            )
        return total

    def put_planes(total, b):
        moved = pltpu.roll(total[:, 2 * chans :], 1, 0)
        moved = jnp.where(colrow == 0, 0.0, moved)
        grads[2 * b] = total[:, :chans] + moved
        grads[2 * b + 1] = total[:, chans : 2 * chans]

    put_planes(back(cot, 1), 1)

    def cut_tile(t, b):
        for par in range(2):
            for jj in range(2):
                gtile32[t, pl.ds(b * 4 + jj * 2 + par, frames, stride=8), :] = grads[
                    2 * b + par, pl.ds(2 * t + jj, frames, stride=half), :
                ]

    loop(0, tpd, lambda t: cut_tile(t, 1), 2)
    upper = back(cot, 0)
    gown[...] = upper

    for i in range(1, nz):
        d = lax.rem(zme + i, nz)
        id_z(d, d).wait_recv()
    every = locr[:, 0, :]
    low = me * tpd
    in_row = (every >= low) & (every < low + tpd)
    got = jnp.broadcast_to(
        jnp.max(jnp.where(in_row, every - low, -1), axis=1, keepdims=True), (ns, 128)
    )
    lane = lax.broadcasted_iota(jnp.int32, (ns, 128), 1)
    who = lax.broadcasted_iota(jnp.int32, (ns, 128), 0)
    src_of = jnp.max(jnp.where(got == lane, who, 0), axis=0, keepdims=True)
    map_v[0:ns, :] = got
    map_v[ns : ns + 8, :] = jnp.broadcast_to(src_of, (8, 128))
    to_scalar = pltpu.make_async_copy(map_v, map_s, in_sem.at[3])
    to_scalar.start()
    to_scalar.wait()

    def wait_tile(i):
        tile_copy(lax.rem(me + i, ns), lax.rem(me + i, ns)).wait_recv()

    loop(1, ns, wait_tile)

    def lay_tile(t):
        tile32[t] = arr[map_s[ns, t]].astype(F32)
        for b in range(2):
            for par in range(2):
                for jj in range(2):
                    planes[2 * b + par, pl.ds(2 * t + jj, frames, stride=half), :] = tile32[
                        t, pl.ds(b * 4 + jj * 2 + par, frames, stride=8), :
                    ]

    loop(0, tpd, lay_tile, 2)

    def next_col(even):
        return jnp.where(colrow == half - 1, 0.0, pltpu.roll(even, fj - 1, 0)).astype(BF)

    def put_rows(b):
        even = planes[2 * b]
        xmat[:, (3 * b) * chans : (3 * b + 1) * chans] = even.astype(BF)
        xmat[:, (3 * b + 1) * chans : (3 * b + 2) * chans] = planes[2 * b + 1].astype(BF)
        xmat[:, (3 * b + 2) * chans : (3 * b + 3) * chans] = next_col(even)

    put_rows(0)

    @pl.when(me > 0)
    def _():
        row_copy.start()

    put_rows(1)

    def weight_grad(b):
        for a in range(3):
            count = fj - (2 - a) * half
            part = lax.dot_general(
                xmat[0:count, 3 * b * chans : 3 * (b + 1) * chans],
                cot[fj - count :, :],
                TN,
                preferred_element_type=F32,
            )
            row = (9 * a + 3 * b) * chans
            gmat[0, row : row + 3 * chans, :] = part[:, :128]
            gmat[1, row : row + 3 * chans, :] = part[:, 128:]

    other = {"dp": 2 * y + 1 - core}

    def core_copy(k, f):
        lo, hi = spans[f]
        return remote(
            cs.at[k, lo:hi], cr.at[k, lo:hi], core_s.at[f, k], core_r.at[f, k], other
        )

    ups = (ny // 2, ny - 1 - ny // 2)
    downs = (ups[1], ups[0])

    def each(f, body):
        for lo, hi, shift in flows[f]:
            loop(lo, hi, lambda q, shift=shift: body(q, q + shift))

    def send_core(f):
        def pack(q, s):
            row = pl.multiple_of(begin(s), 16)
            window = gmat[1 - core, pl.ds(row, rc * ny), :].astype(BF)
            cs[:, q] = window.reshape(ny, rc, 128)

        each(f, pack)
        for i in range(max(ups[f], downs[f])):
            if i < ups[f]:
                core_copy(lax.rem(y + ups[f] - i, ny), f).start()
            if i < downs[f]:
                core_copy(lax.rem(y + ny - downs[f] + i, ny), f).start()
        core_copy(y, f).start()

    def mine(k, q, s):
        row = pl.multiple_of(begin(s) + rc * k, 16)
        return gmat[core, pl.ds(row, rc), :] + cr[k, q].astype(F32)

    up = {"dp": 2 * lax.rem(y + 1, ny) + core}
    down = {"dp": 2 * lax.rem(y + ny - 1, ny) + core}

    def up_copy(i, f, r):
        lo, hi, _ = flows[f][r]
        n = sum(len(flow) for flow in flows[:f]) + r
        return remote(cws.at[i, lo:hi], cwr.at[i, lo:hi], cw_s.at[n, i], cw_r.at[n, i], up)

    def down_copy(i, f, r):
        lo, hi, _ = flows[f][r]
        n = sum(len(flow) for flow in flows[:f]) + r
        return remote(ccs.at[i, lo:hi], ccr.at[i, lo:hi], cc_s.at[n, i], cc_r.at[n, i], down)

    def hop(k, i, f, r, send, into, out_of):
        lo, hi, shift = flows[f][r]
        if i > 0:
            send(i - 1, f, r).wait_recv()

        def add(q):
            v = mine(k, q, q + shift)
            if i > 0:
                v = v + out_of[i - 1, q].astype(F32)
            into[i, q] = v.astype(BF)

        loop(lo, hi, add)
        send(i, f, r).start()

    def chain(f, i):
        k_up = lax.rem(y + ups[f] - i + ny, ny)
        k_down = lax.rem(y + ny - downs[f] + i, ny)
        if i < ups[f]:
            core_copy(k_up, f).wait_recv()
        if i < downs[f]:
            core_copy(k_down, f).wait_recv()
        for r in range(len(flows[f])):
            if i < ups[f]:
                hop(k_up, i, f, r, up_copy, cws, cwr)
            if i < downs[f]:
                hop(k_down, i, f, r, down_copy, ccs, ccr)

    weight_grad(1)
    weight_grad(0)

    @pl.when(core == 1)
    def _():
        pl.semaphore_wait(late_sem, ny)

    send_core(0)

    @pl.when(me > 0)
    def _():
        cot_copy.wait_recv()

    put_planes(gown[...] + back(cotprev, 2), 0)

    def cut_upper(t):
        cut_tile(t, 0)
        tiles[t] = gtile32[t].astype(BF)

    loop(0, tpd, cut_upper, 2)

    chain(0, 0)

    def back_copy(d, s):
        return remote(stage2.at[d], ret.at[s], rt_s.at[d], rt_r.at[s], {"space": d})

    def send_back(i):
        d = lax.rem(me + i, ns)
        stage2[d] = tiles[jnp.maximum(map_s[d, 0], 0)]
        back_copy(d, me).start()

    loop(1, ns, send_back)
    ret[me] = tiles[jnp.maximum(map_s[me, 0], 0)]

    @pl.when(me < ns - 1)
    def _():
        row_copy.wait_recv()

    xmat[:, 8 * chans : 9 * chans] = next_col(
        xmat[:, 6 * chans : 7 * chans].astype(F32)
    )
    weight_grad(2)
    send_core(1)
    chain(0, 1)
    chain(1, 0)

    for i in range(2, max(ups)):
        chain(0, i)
        chain(1, i - 1)

    def sp_copy(d, s):
        return remote(spst.at[d], spr.at[s], sp_s.at[d], sp_r.at[s], {"space": d})

    def spread(f):
        core_copy(y, f).wait_recv()
        for r, (lo, hi, shift) in enumerate(flows[f]):
            for send, steps in ((up_copy, ups), (down_copy, downs)):
                if steps[f] > 0:
                    send(steps[f] - 1, f, r).wait_recv()

            def part(q, shift=shift):
                s = q + shift
                v = mine(y, q, s)
                for landed, steps in ((cwr, ups), (ccr, downs)):
                    if steps[f] > 0:
                        v = v + landed[steps[f] - 1, q].astype(F32)
                spst[s] = v.astype(BF)

                @pl.when(s != me)
                def _():
                    sp_copy(s, me).start()

            loop(lo, hi, part)

    def done_tiles(i):
        tile_copy(lax.rem(me + i, ns), me).wait_send()

    loop(1, ns, done_tiles)
    for i in range(1, nx):
        id_x(lax.rem(xme + i, nx), xme).wait_send()
    for i in range(1, nz):
        id_z(lax.rem(zme + i, nz), zme).wait_send()

    @pl.when(me < ns - 1)
    def _():
        cot_copy.wait_send()

    @pl.when(me > 0)
    def _():
        row_copy.wait_send()

    spread(0)
    chain(1, max(ups) - 1)
    spread(1)
    spr[me] = spst[me]

    def done_core(k):
        for f in range(2):
            core_copy(k, f).wait_send()

    loop(0, ny, done_core)
    for f in range(2):
        for r in range(len(flows[f])):
            for i in range(ups[f]):
                up_copy(i, f, r).wait_send()
            for i in range(downs[f]):
                down_copy(i, f, r).wait_send()

    total = lax.dot_general(xmat[...], weight[18 * chans :, :], NN, preferred_element_type=F32)
    for a in (1, 0):
        skip = (2 - a) * half
        part = lax.dot_general(
            xmat[0 : fj - skip, :],
            weight[9 * a * chans : 9 * (a + 1) * chans, :],
            NN,
            preferred_element_type=F32,
        )
        total = total + jnp.concatenate([jnp.zeros((skip, 256), F32), part], axis=0)
    out[...] = total.astype(BF)

    def wait_back(i):
        back_copy(lax.rem(me + i, ns), lax.rem(me + i, ns)).wait_recv()
        back_copy(lax.rem(me + i, ns), me).wait_send()

    loop(1, ns, wait_back)

    def pull(k):
        tile = owners[k]
        g = ret[jnp.minimum(tile // tpd, ns - 1)].astype(F32)
        g = jnp.where(tile < tpd * ns, g, 0.0)
        n, scale = normed(clips[k].astype(F32))
        v = n * gam
        sig = 0.5 + 0.5 * jnp.tanh(0.5 * v)
        dn = g * sig * (1.0 + v * (1.0 - sig)) * gam
        gin[k] = (scale * (dn - n * jnp.mean(dn * n, axis=-1, keepdims=True))).astype(BF)

    middle = clips.shape[0] // 2
    loop(0, middle, pull, 4)

    def wait_sp(i):
        sp_copy(lax.rem(me + i, ns), lax.rem(me + i, ns)).wait_recv()

    loop(1, ns, wait_sp)
    finr[core, y] = jnp.sum(spr[...].astype(F32), axis=0).astype(BF)

    def ag_copy(d, s):
        slot = finr.at[lax.rem(s, 2), s // 2]
        return remote(slot, slot, ag_s.at[d], ag_r.at[s], {"dp": d})

    def send_ag(i):
        ag_copy(lax.rem(dp + i, ndp), dp).start()

    loop(1, ndp, send_ag)

    loop(middle, clips.shape[0], pull, 4)

    def done_sp(i):
        sp_copy(lax.rem(me + i, ns), me).wait_send()

    loop(1, ns, done_sp)

    def wait_ag(i):
        d = lax.rem(dp + i, ndp)
        ag_copy(d, d).wait_recv()

    loop(1, ndp, wait_ag)
    for off in range(0, 16, 4):

        @pl.when(me * wrows - begin(me) == off)
        def _(off=off):
            for h in range(2):
                window = finr[h].reshape(ny * rc, 128).astype(F32)
                fin[:, h * 128 : (h + 1) * 128] = window[off : off + wrows]

    def done_dp(i):
        ag_copy(lax.rem(dp + i, ndp), dp).wait_send()

    loop(1, ndp, done_dp)


def pin(x):
    return pltpu.with_memory_space_constraint(x, pltpu.HBM)


def flows(ns, wrows):
    kinds = [[], []]
    for s in range(ns):
        taps = range(s * wrows // 128, (s * wrows + wrows - 1) // 128 + 1)
        kinds[1 if any((tap % 9) // 3 == 2 for tap in taps) else 0].append(s)
    found = []
    q = 0
    for kind in kinds:
        ranges = []
        for s in kind:
            if ranges and ranges[-1][1] + ranges[-1][2] == s:
                ranges[-1] = (ranges[-1][0], q + 1, ranges[-1][2])
            else:
                ranges.append((q, q + 1, s - q))
            q += 1
        found.append(tuple(ranges))
    return tuple(found)


def local(clips, a_tile, gamma, weight, cotangent):
    ns = lax.axis_size("space")
    ny = lax.axis_size("dp") // 2
    frames, rows_in, tcols, chans = clips.shape[2:]
    half = cotangent.shape[3]
    tpd = half // 2
    cap = clips.shape[1]
    fj = frames * half
    trows = frames * rows_in * tcols
    wrows = weight.shape[0] // ns
    nx = 4
    ranges = sum(len(flow) for flow in flows(ns, wrows))
    rc = 16 * -(-(wrows + 12) // (16 * ny))
    pad = max(((s * wrows) // 16) * 16 + rc * ny for s in range(ns))
    vmem = pl.BlockSpec(memory_space=pltpu.VMEM)
    smem = pl.BlockSpec(memory_space=pltpu.SMEM)
    hbm = pl.BlockSpec(memory_space=pltpu.HBM)
    dma = pltpu.SemaphoreType.DMA
    tiles_shape = pltpu.VMEM((ns, trows, chans), BF)
    reach = ny // 2
    piece = (ns, rc, 128)
    out, gin, fin = pl.pallas_call(
        functools.partial(kernel, (ns, nx, ny, frames, half, wrows, rc, flows(ns, wrows))),
        out_shape=(
            jax.ShapeDtypeStruct((fj, 256), BF),
            jax.ShapeDtypeStruct((cap, trows, chans), BF),
            jax.ShapeDtypeStruct((wrows, 256), F32),
        ),
        in_specs=[smem, vmem, hbm, vmem, hbm, hbm],
        out_specs=(vmem, vmem, vmem),
        scratch_shapes=[
            pltpu.VMEM((cap, trows, chans), BF),
            pltpu.VMEM(weight.shape, BF),
            pltpu.VMEM((fj, 256), BF),
            pltpu.VMEM((fj, 256), BF),
            pltpu.VMEM((cap, trows, chans), BF),
            pltpu.VMEM((ns, 128), jnp.int32),
            pltpu.SMEM((ns, 128), jnp.int32),
            tiles_shape,
            tiles_shape,
            tiles_shape,
            tiles_shape,
            pltpu.VMEM((ns, 1, 128), jnp.int32),
            pltpu.VMEM((ns + 8, 128), jnp.int32),
            pltpu.SMEM((ns + 8, 128), jnp.int32),
            pltpu.VMEM((tpd, trows, chans), F32),
            pltpu.VMEM((tpd, trows, chans), BF),
            pltpu.VMEM((4, fj, chans), F32),
            pltpu.VMEM((4, fj, chans), F32),
            pltpu.VMEM((fj, 3 * chans), F32),
            pltpu.VMEM((tpd, trows, chans), F32),
            pltpu.VMEM((fj, 9 * chans), BF),
            pltpu.VMEM((2, pad, 128), F32),
            pltpu.VMEM((ny,) + piece, BF),
            pltpu.VMEM((ny,) + piece, BF),
            pltpu.VMEM((reach,) + piece, BF),
            pltpu.VMEM((reach,) + piece, BF),
            pltpu.VMEM((reach,) + piece, BF),
            pltpu.VMEM((reach,) + piece, BF),
            pltpu.VMEM(piece, BF),
            pltpu.VMEM(piece, BF),
            pltpu.VMEM((2, ny, rc, 128), BF),
            dma((5,)),
            dma((nx + ns // nx,)),
            dma((nx + ns // nx,)),
            dma((ns,)),
            dma((ns,)),
            dma((ns,)),
            dma((ns,)),
            dma((2,)),
            dma((2,)),
            dma((2, ny)),
            dma((2, ny)),
            dma((ranges, reach)),
            dma((ranges, reach)),
            dma((ranges, reach)),
            dma((ranges, reach)),
            dma((ns,)),
            dma((ns,)),
            dma((2 * ny,)),
            dma((2 * ny,)),
            pltpu.SemaphoreType.REGULAR,
        ],
        compiler_params=pltpu.CompilerParams(
            collective_id=0, has_side_effects=True, vmem_limit_bytes=48 * 1024 * 1024
        ),
    )(
        pin(a_tile[0]),
        pin(a_tile),
        pin(clips.reshape(cap, trows, chans)),
        pin(gamma.reshape(1, chans)),
        pin(weight),
        pin(cotangent.reshape(fj, 256)),
    )
    return (
        out.reshape(1, frames, 1, half, 256),
        gin.reshape(clips.shape),
        fin,
    )


def solution(mesh):
    return jax.shard_map(
        local,
        mesh=mesh,
        in_specs=(
            P("dp", "space", None, None, None, None),
            P("dp", "space"),
            P(),
            P(),
            P("dp", None, "space", None, None),
        ),
        out_specs=(
            P("dp", None, "space", None, None),
            P("dp", "space", None, None, None, None),
            P("space", None),
        ),
        check_vma=False,
    )
```

```python
import functools

import jax
import jax.numpy as jnp
from jax import lax
from jax.experimental import pallas as pl
from jax.experimental.pallas import tpu as pltpu
from jax.sharding import PartitionSpec as P

TPD = 16
BF = jnp.bfloat16
F32 = jnp.float32
NN = (((1,), (0,)), ((), ()))
NT = (((1,), (1,)), ((), ()))
TN = (((0,), (0,)), ((), ()))


def remote(src, dst, ssem, rsem, dev):
    return pltpu.make_async_remote_copy(
        src_ref=src,
        dst_ref=dst,
        send_sem=ssem,
        recv_sem=rsem,
        device_id=dev,
        device_id_type=pl.DeviceIdType.MESH,
    )


def loop(lo, hi, body, unroll=1):
    def step(i, carry):
        body(i)
        return carry

    lax.fori_loop(lo, hi, step, 0, unroll=unroll)


def normed(x):
    meansq = jnp.mean(x * x, axis=-1, keepdims=True)
    scale = lax.rsqrt(meansq + 1e-06)
    return x * scale, scale


def kernel(
    dims,
    owners,
    ids,
    clips_h,
    gamma,
    weight_h,
    cot_h,
    out,
    gin,
    fin,
    clips,
    weight,
    cot,
    cotprev,
    hid,
    slot_v,
    slot_s,
    stage,
    arr,
    stage2,
    ret,
    locr,
    map_v,
    map_s,
    tile32,
    tiles,
    planes,
    grads,
    gown,
    gtile32,
    xmat,
    gmat,
    cs,
    cr,
    cws,
    cwr,
    ccs,
    ccr,
    spst,
    spr,
    finr,
    in_sem,
    id_s,
    id_r,
    st_s,
    st_r,
    rt_s,
    rt_r,
    hop_s,
    hop_r,
    core_s,
    core_r,
    cw_s,
    cw_r,
    cc_s,
    cc_r,
    sp_s,
    sp_r,
    ag_s,
    ag_r,
    late_sem,
):
    ns, nx, ny, frames, half, wrows, rc, flows = dims
    spans = [(f[0][0], f[-1][1]) for f in flows]
    ndp = 2 * ny
    chans = 128
    tpd = half // 2
    me = lax.axis_index("space")
    dp = lax.axis_index("dp")
    y = dp // 2
    core = lax.rem(dp, 2)
    fj = frames * half

    def begin(k):
        return ((k * wrows) // 16) * 16

    loads = [
        pltpu.make_async_copy(clips_h, clips, in_sem.at[0]),
        pltpu.make_async_copy(cot_h, cot, in_sem.at[1]),
        pltpu.make_async_copy(weight_h, weight, in_sem.at[2]),
    ]
    for load in loads:
        load.start()
    barrier = pltpu.get_barrier_semaphore()

    def greet_space(i):
        pl.semaphore_signal(
            barrier,
            inc=1,
            device_id={"space": lax.rem(me + i, ns)},
            device_id_type=pl.DeviceIdType.MESH,
        )

    def greet_dp(sem, j, other_core):
        pl.semaphore_signal(
            sem,
            inc=1,
            device_id={"dp": 2 * j + other_core},
            device_id_type=pl.DeviceIdType.MESH,
        )

    loop(1, ny, lambda i: greet_dp(barrier, lax.rem(y + i, ny), core))

    @pl.when(core == 1)
    def _():
        loop(0, ny, lambda j: greet_dp(barrier, j, 0))

    loop(1, ns, greet_space)

    @pl.when(me == 0)
    def _():
        cotprev[...] = jnp.zeros(cotprev.shape, BF)

    @pl.when(me == ns - 1)
    def _():
        xmat[:, 6 * chans : 8 * chans] = jnp.zeros((fj, 2 * chans), BF)

    gmat[:, 27 * chans :, :] = jnp.zeros((2, gmat.shape[1] - 27 * chans, 128), F32)
    shape = (ns, 128)
    none = jnp.full((1, 128 - ids.shape[1]), tpd * ns, jnp.int32)
    id_row = jnp.concatenate([ids[...], none], axis=1)
    own_ids = jnp.broadcast_to(id_row, shape)
    first_id = lax.broadcasted_iota(jnp.int32, shape, 0) * tpd
    match = (own_ids >= first_id) & (own_ids < first_id + tpd)
    slots = lax.broadcasted_iota(jnp.int32, shape, 1)
    slot_of = jnp.max(jnp.where(match, slots, 0), axis=1, keepdims=True)
    slot_of = jnp.minimum(slot_of, clips.shape[0] - 1)
    slot_v[...] = jnp.broadcast_to(slot_of, (ns, 128))
    locr[me] = id_row
    slot_copy = pltpu.make_async_copy(slot_v, slot_s, in_sem.at[4])
    slot_copy.start()

    gam = gamma[...]
    loads[0].wait()

    gam_half = gam * 0.5

    def hide(k):
        x = clips[k].astype(F32)
        h = x * lax.rsqrt(jnp.mean(x * x, axis=-1, keepdims=True) + 1e-06) * gam_half
        hid[k] = (h + h * jnp.tanh(h)).astype(BF)

    loop(0, clips.shape[0], hide, 4)
    slot_copy.wait()

    def set_out(d):
        stage[d] = hid[slot_s[d, 0]]

    loop(0, ns, set_out, 4)
    arr[me] = stage[me]
    loads[1].wait()
    pl.semaphore_wait(barrier, ns - 1 + ny - 1 + ny * (1 - core))

    zme = me // nx
    xme = lax.rem(me, nx)
    nz = ns // nx

    def id_x(d, s):
        return remote(
            locr.at[zme * nx + s], locr.at[zme * nx + s], id_s.at[d], id_r.at[s],
            {"space": zme * nx + d},
        )

    def id_z(d, s):
        rows = locr.at[pl.ds(s * nx, nx)]
        return remote(
            rows, rows, id_s.at[nx + d], id_r.at[nx + s], {"space": d * nx + xme}
        )

    def tile_copy(d, s):
        return remote(stage.at[d], arr.at[s], st_s.at[d], st_r.at[s], {"space": d})

    for i in range(1, nx):
        id_x(lax.rem(xme + i, nx), xme).start()

    above = lax.rem(me + ns - 1, ns)
    under = lax.rem(me + 1, ns)
    cot_copy = remote(cot, cotprev, hop_s.at[0], hop_r.at[0], {"space": under})
    row_copy = remote(
        xmat.at[:, 0 : 2 * chans],
        xmat.at[:, 6 * chans : 8 * chans],
        hop_s.at[1],
        hop_r.at[1],
        {"space": above},
    )

    def send_tile(i):
        tile_copy(lax.rem(me + i, ns), me).start()

    loop(1, ns, send_tile)

    @pl.when(core == 0)
    def _():
        loop(0, ny, lambda j: greet_dp(late_sem, j, 1))

    for i in range(1, nx):
        d = lax.rem(xme + i, nx)
        id_x(d, d).wait_recv()
    for i in range(1, nz):
        id_z(lax.rem(zme + i, nz), zme).start()

    loads[2].wait()
    colrow = lax.rem(lax.broadcasted_iota(jnp.int32, (fj, chans), 0), half)

    def wpart(a, b):
        return weight[pl.ds((a * 9 + b * 3) * chans, 3 * chans), :]

    def back(source, b):
        total = lax.dot_general(source[...], wpart(2, b), NT, preferred_element_type=F32)
        for a in (1, 0):
            skip = (2 - a) * half
            part = lax.dot_general(
                source[skip:, :], wpart(a, b), NT, preferred_element_type=F32
            )
            total = total + jnp.concatenate(
                [part, jnp.zeros((skip, 3 * chans), F32)], axis=0
            )
        return total

    def put_planes(total, b):
        moved = pltpu.roll(total[:, 2 * chans :], 1, 0)
        moved = jnp.where(colrow == 0, 0.0, moved)
        grads[2 * b] = total[:, :chans] + moved
        grads[2 * b + 1] = total[:, chans : 2 * chans]

    put_planes(back(cot, 1), 1)

    def cut_tile(t, b):
        for par in range(2):
            for jj in range(2):
                gtile32[t, pl.ds(b * 4 + jj * 2 + par, frames, stride=8), :] = grads[
                    2 * b + par, pl.ds(2 * t + jj, frames, stride=half), :
                ]

    loop(0, tpd, lambda t: cut_tile(t, 1), 2)
    upper = back(cot, 0)
    gown[...] = upper

    for i in range(1, nz):
        d = lax.rem(zme + i, nz)
        id_z(d, d).wait_recv()
    every = locr[:, 0, :]
    low = me * tpd
    in_row = (every >= low) & (every < low + tpd)
    got = jnp.broadcast_to(
        jnp.max(jnp.where(in_row, every - low, -1), axis=1, keepdims=True), (ns, 128)
    )
    lane = lax.broadcasted_iota(jnp.int32, (ns, 128), 1)
    who = lax.broadcasted_iota(jnp.int32, (ns, 128), 0)
    src_of = jnp.max(jnp.where(got == lane, who, 0), axis=0, keepdims=True)
    map_v[0:ns, :] = got
    map_v[ns : ns + 8, :] = jnp.broadcast_to(src_of, (8, 128))
    to_scalar = pltpu.make_async_copy(map_v, map_s, in_sem.at[3])
    to_scalar.start()
    to_scalar.wait()

    def wait_tile(i):
        tile_copy(lax.rem(me + i, ns), lax.rem(me + i, ns)).wait_recv()

    loop(1, ns // 2, wait_tile)

    @pl.when(me < ns - 1)
    def _():
        cot_copy.start()

    loop(ns // 2, ns, wait_tile)

    def lay_tile(t):
        tile32[t] = arr[map_s[ns, t]].astype(F32)
        for b in range(2):
            for par in range(2):
                for jj in range(2):
                    planes[2 * b + par, pl.ds(2 * t + jj, frames, stride=half), :] = tile32[
                        t, pl.ds(b * 4 + jj * 2 + par, frames, stride=8), :
                    ]

    loop(0, tpd, lay_tile, 2)

    def next_col(even):
        return jnp.where(colrow == half - 1, 0.0, pltpu.roll(even, fj - 1, 0)).astype(BF)

    def put_rows(b):
        even = planes[2 * b]
        xmat[:, (3 * b) * chans : (3 * b + 1) * chans] = even.astype(BF)
        xmat[:, (3 * b + 1) * chans : (3 * b + 2) * chans] = planes[2 * b + 1].astype(BF)
        xmat[:, (3 * b + 2) * chans : (3 * b + 3) * chans] = next_col(even)

    put_rows(0)

    @pl.when(me > 0)
    def _():
        row_copy.start()

    put_rows(1)

    def weight_grad(b):
        for a in range(3):
            count = fj - (2 - a) * half
            part = lax.dot_general(
                xmat[0:count, 3 * b * chans : 3 * (b + 1) * chans],
                cot[fj - count :, :],
                TN,
                preferred_element_type=F32,
            )
            row = (9 * a + 3 * b) * chans
            gmat[0, row : row + 3 * chans, :] = part[:, :128]
            gmat[1, row : row + 3 * chans, :] = part[:, 128:]

    other = {"dp": 2 * y + 1 - core}

    def core_copy(k, f):
        lo, hi = spans[f]
        return remote(
            cs.at[k, lo:hi], cr.at[k, lo:hi], core_s.at[f, k], core_r.at[f, k], other
        )

    ups = (ny // 2, ny - 1 - ny // 2)
    downs = (ups[1], ups[0])

    def each(f, body):
        for lo, hi, shift in flows[f]:
            loop(lo, hi, lambda q, shift=shift: body(q, q + shift))

    def send_core(f):
        def pack(q, s):
            row = pl.multiple_of(begin(s), 16)
            window = gmat[1 - core, pl.ds(row, rc * ny), :].astype(BF)
            cs[:, q] = window.reshape(ny, rc, 128)

        each(f, pack)
        for i in range(max(ups[f], downs[f])):
            if i < ups[f]:
                core_copy(lax.rem(y + ups[f] - i, ny), f).start()
            if i < downs[f]:
                core_copy(lax.rem(y + ny - downs[f] + i, ny), f).start()
        core_copy(y, f).start()

    def mine(k, q, s):
        row = pl.multiple_of(begin(s) + rc * k, 16)
        return gmat[core, pl.ds(row, rc), :] + cr[k, q].astype(F32)

    up = {"dp": 2 * lax.rem(y + 1, ny) + core}
    down = {"dp": 2 * lax.rem(y + ny - 1, ny) + core}

    def up_copy(i, f, r):
        lo, hi, _ = flows[f][r]
        n = sum(len(flow) for flow in flows[:f]) + r
        return remote(cws.at[i, lo:hi], cwr.at[i, lo:hi], cw_s.at[n, i], cw_r.at[n, i], up)

    def down_copy(i, f, r):
        lo, hi, _ = flows[f][r]
        n = sum(len(flow) for flow in flows[:f]) + r
        return remote(ccs.at[i, lo:hi], ccr.at[i, lo:hi], cc_s.at[n, i], cc_r.at[n, i], down)

    def hop(k, i, f, r, send, into, out_of):
        lo, hi, shift = flows[f][r]
        if i > 0:
            send(i - 1, f, r).wait_recv()

        def add(q):
            v = mine(k, q, q + shift)
            if i > 0:
                v = v + out_of[i - 1, q].astype(F32)
            into[i, q] = v.astype(BF)

        loop(lo, hi, add)
        send(i, f, r).start()

    def chain(f, i):
        k_up = lax.rem(y + ups[f] - i + ny, ny)
        k_down = lax.rem(y + ny - downs[f] + i, ny)
        if i < ups[f]:
            core_copy(k_up, f).wait_recv()
        if i < downs[f]:
            core_copy(k_down, f).wait_recv()
        for r in range(len(flows[f])):
            if i < ups[f]:
                hop(k_up, i, f, r, up_copy, cws, cwr)
            if i < downs[f]:
                hop(k_down, i, f, r, down_copy, ccs, ccr)

    weight_grad(1)
    weight_grad(0)

    @pl.when(core == 1)
    def _():
        pl.semaphore_wait(late_sem, ny)

    send_core(0)
    chain(0, 0)

    @pl.when(me > 0)
    def _():
        cot_copy.wait_recv()

    put_planes(gown[...] + back(cotprev, 2), 0)

    def cut_upper(t):
        cut_tile(t, 0)
        tiles[t] = gtile32[t].astype(BF)

    loop(0, tpd, cut_upper, 2)

    def back_copy(d, s):
        return remote(stage2.at[d], ret.at[s], rt_s.at[d], rt_r.at[s], {"space": d})

    def send_back(i):
        d = lax.rem(me + i, ns)
        stage2[d] = tiles[jnp.maximum(map_s[d, 0], 0)]
        back_copy(d, me).start()

    loop(1, ns, send_back)
    ret[me] = tiles[jnp.maximum(map_s[me, 0], 0)]

    @pl.when(me < ns - 1)
    def _():
        row_copy.wait_recv()

    xmat[:, 8 * chans : 9 * chans] = next_col(
        xmat[:, 6 * chans : 7 * chans].astype(F32)
    )
    weight_grad(2)
    send_core(1)
    chain(0, 1)
    chain(1, 0)

    for i in range(2, max(ups)):
        chain(0, i)
        chain(1, i - 1)

    def sp_copy(d, s):
        return remote(spst.at[d], spr.at[s], sp_s.at[d], sp_r.at[s], {"space": d})

    def spread(f):
        core_copy(y, f).wait_recv()
        for r, (lo, hi, shift) in enumerate(flows[f]):
            for send, steps in ((up_copy, ups), (down_copy, downs)):
                if steps[f] > 0:
                    send(steps[f] - 1, f, r).wait_recv()

            def part(q, shift=shift):
                s = q + shift
                v = mine(y, q, s)
                for landed, steps in ((cwr, ups), (ccr, downs)):
                    if steps[f] > 0:
                        v = v + landed[steps[f] - 1, q].astype(F32)
                spst[s] = v.astype(BF)

                @pl.when(s != me)
                def _():
                    sp_copy(s, me).start()

            loop(lo, hi, part)

    def done_tiles(i):
        tile_copy(lax.rem(me + i, ns), me).wait_send()

    loop(1, ns, done_tiles)
    for i in range(1, nx):
        id_x(lax.rem(xme + i, nx), xme).wait_send()
    for i in range(1, nz):
        id_z(lax.rem(zme + i, nz), zme).wait_send()

    @pl.when(me < ns - 1)
    def _():
        cot_copy.wait_send()

    @pl.when(me > 0)
    def _():
        row_copy.wait_send()

    spread(0)
    chain(1, max(ups) - 1)
    spread(1)
    spr[me] = spst[me]

    def done_core(k):
        for f in range(2):
            core_copy(k, f).wait_send()

    loop(0, ny, done_core)
    for f in range(2):
        for r in range(len(flows[f])):
            for i in range(ups[f]):
                up_copy(i, f, r).wait_send()
            for i in range(downs[f]):
                down_copy(i, f, r).wait_send()

    total = lax.dot_general(xmat[...], weight[18 * chans :, :], NN, preferred_element_type=F32)
    for a in (1, 0):
        skip = (2 - a) * half
        part = lax.dot_general(
            xmat[0 : fj - skip, :],
            weight[9 * a * chans : 9 * (a + 1) * chans, :],
            NN,
            preferred_element_type=F32,
        )
        total = total + jnp.concatenate([jnp.zeros((skip, 256), F32), part], axis=0)
    out[...] = total.astype(BF)

    def wait_back(i):
        back_copy(lax.rem(me + i, ns), lax.rem(me + i, ns)).wait_recv()
        back_copy(lax.rem(me + i, ns), me).wait_send()

    loop(1, ns, wait_back)

    def pull(k):
        tile = owners[k]
        g = ret[jnp.minimum(tile // tpd, ns - 1)].astype(F32)
        g = jnp.where(tile < tpd * ns, g, 0.0)
        n, scale = normed(clips[k].astype(F32))
        v = n * gam
        sig = 0.5 + 0.5 * jnp.tanh(0.5 * v)
        dn = g * sig * (1.0 + v * (1.0 - sig)) * gam
        gin[k] = (scale * (dn - n * jnp.mean(dn * n, axis=-1, keepdims=True))).astype(BF)

    middle = clips.shape[0] // 2
    loop(0, middle, pull, 4)

    def wait_sp(i):
        sp_copy(lax.rem(me + i, ns), lax.rem(me + i, ns)).wait_recv()

    loop(1, ns, wait_sp)
    finr[core, y] = jnp.sum(spr[...].astype(F32), axis=0).astype(BF)

    def ag_copy(d, s):
        slot = finr.at[lax.rem(s, 2), s // 2]
        return remote(slot, slot, ag_s.at[d], ag_r.at[s], {"dp": d})

    def send_ag(i):
        ag_copy(lax.rem(dp + i, ndp), dp).start()

    loop(1, ndp, send_ag)

    loop(middle, clips.shape[0], pull, 4)

    def done_sp(i):
        sp_copy(lax.rem(me + i, ns), me).wait_send()

    loop(1, ns, done_sp)

    def wait_ag(i):
        d = lax.rem(dp + i, ndp)
        ag_copy(d, d).wait_recv()

    loop(1, ndp, wait_ag)
    for off in range(0, 16, 4):

        @pl.when(me * wrows - begin(me) == off)
        def _(off=off):
            for h in range(2):
                window = finr[h].reshape(ny * rc, 128).astype(F32)
                fin[:, h * 128 : (h + 1) * 128] = window[off : off + wrows]

    def done_dp(i):
        ag_copy(lax.rem(dp + i, ndp), dp).wait_send()

    loop(1, ndp, done_dp)


def pin(x):
    return pltpu.with_memory_space_constraint(x, pltpu.HBM)


def settle(out, gin, fin, out_to, gin_to, fin_to, sem):
    pairs = ((out, out_to), (gin, gin_to), (fin, fin_to))
    copies = [pltpu.make_async_copy(a, b, sem.at[i]) for i, (a, b) in enumerate(pairs)]
    for copy in copies:
        copy.start()
    for copy in copies:
        copy.wait()


def flows(ns, wrows):
    kinds = [[], []]
    for s in range(ns):
        taps = range(s * wrows // 128, (s * wrows + wrows - 1) // 128 + 1)
        kinds[1 if any((tap % 9) // 3 == 2 for tap in taps) else 0].append(s)
    found = []
    q = 0
    for kind in kinds:
        ranges = []
        for s in kind:
            if ranges and ranges[-1][1] + ranges[-1][2] == s:
                ranges[-1] = (ranges[-1][0], q + 1, ranges[-1][2])
            else:
                ranges.append((q, q + 1, s - q))
            q += 1
        found.append(tuple(ranges))
    return tuple(found)


def local(clips, a_tile, gamma, weight, cotangent):
    ns = lax.axis_size("space")
    ny = lax.axis_size("dp") // 2
    frames, rows_in, tcols, chans = clips.shape[2:]
    half = cotangent.shape[3]
    tpd = half // 2
    cap = clips.shape[1]
    fj = frames * half
    trows = frames * rows_in * tcols
    wrows = weight.shape[0] // ns
    nx = 4
    ranges = sum(len(flow) for flow in flows(ns, wrows))
    rc = 16 * -(-(wrows + 12) // (16 * ny))
    pad = max(((s * wrows) // 16) * 16 + rc * ny for s in range(ns))
    vmem = pl.BlockSpec(memory_space=pltpu.VMEM)
    smem = pl.BlockSpec(memory_space=pltpu.SMEM)
    hbm = pl.BlockSpec(memory_space=pltpu.HBM)
    dma = pltpu.SemaphoreType.DMA
    tiles_shape = pltpu.VMEM((ns, trows, chans), BF)
    reach = ny // 2
    piece = (ns, rc, 128)
    out, gin, fin = pl.pallas_call(
        functools.partial(kernel, (ns, nx, ny, frames, half, wrows, rc, flows(ns, wrows))),
        out_shape=(
            jax.ShapeDtypeStruct((fj, 256), BF),
            jax.ShapeDtypeStruct((cap, trows, chans), BF),
            jax.ShapeDtypeStruct((wrows, 256), F32),
        ),
        in_specs=[smem, vmem, hbm, vmem, hbm, hbm],
        out_specs=(vmem, vmem, vmem),
        scratch_shapes=[
            pltpu.VMEM((cap, trows, chans), BF),
            pltpu.VMEM(weight.shape, BF),
            pltpu.VMEM((fj, 256), BF),
            pltpu.VMEM((fj, 256), BF),
            pltpu.VMEM((cap, trows, chans), BF),
            pltpu.VMEM((ns, 128), jnp.int32),
            pltpu.SMEM((ns, 128), jnp.int32),
            tiles_shape,
            tiles_shape,
            tiles_shape,
            tiles_shape,
            pltpu.VMEM((ns, 1, 128), jnp.int32),
            pltpu.VMEM((ns + 8, 128), jnp.int32),
            pltpu.SMEM((ns + 8, 128), jnp.int32),
            pltpu.VMEM((tpd, trows, chans), F32),
            pltpu.VMEM((tpd, trows, chans), BF),
            pltpu.VMEM((4, fj, chans), F32),
            pltpu.VMEM((4, fj, chans), F32),
            pltpu.VMEM((fj, 3 * chans), F32),
            pltpu.VMEM((tpd, trows, chans), F32),
            pltpu.VMEM((fj, 9 * chans), BF),
            pltpu.VMEM((2, pad, 128), F32),
            pltpu.VMEM((ny,) + piece, BF),
            pltpu.VMEM((ny,) + piece, BF),
            pltpu.VMEM((reach,) + piece, BF),
            pltpu.VMEM((reach,) + piece, BF),
            pltpu.VMEM((reach,) + piece, BF),
            pltpu.VMEM((reach,) + piece, BF),
            pltpu.VMEM(piece, BF),
            pltpu.VMEM(piece, BF),
            pltpu.VMEM((2, ny, rc, 128), BF),
            dma((5,)),
            dma((nx + ns // nx,)),
            dma((nx + ns // nx,)),
            dma((ns,)),
            dma((ns,)),
            dma((ns,)),
            dma((ns,)),
            dma((2,)),
            dma((2,)),
            dma((2, ny)),
            dma((2, ny)),
            dma((ranges, reach)),
            dma((ranges, reach)),
            dma((ranges, reach)),
            dma((ranges, reach)),
            dma((ns,)),
            dma((ns,)),
            dma((2 * ny,)),
            dma((2 * ny,)),
            pltpu.SemaphoreType.REGULAR,
        ],
        compiler_params=pltpu.CompilerParams(
            collective_id=0, has_side_effects=True, vmem_limit_bytes=48 * 1024 * 1024
        ),
    )(
        pin(a_tile[0]),
        pin(a_tile),
        pin(clips.reshape(cap, trows, chans)),
        pin(gamma.reshape(1, chans)),
        pin(weight),
        pin(cotangent.reshape(fj, 256)),
    )
    any_ = pl.BlockSpec(memory_space=pl.ANY)
    out, gin, fin = pl.pallas_call(
        settle,
        out_shape=tuple(jax.ShapeDtypeStruct(v.shape, v.dtype) for v in (out, gin, fin)),
        in_specs=[vmem] * 3,
        out_specs=(any_,) * 3,
        scratch_shapes=[dma((3,))],
    )(*(pltpu.with_memory_space_constraint(v, pltpu.VMEM) for v in (out, gin, fin)))
    return (
        out.reshape(1, frames, 1, half, 256),
        gin.reshape(clips.shape),
        fin,
    )


def solution(mesh):
    return jax.shard_map(
        local,
        mesh=mesh,
        in_specs=(
            P("dp", "space", None, None, None, None),
            P("dp", "space"),
            P(),
            P(),
            P("dp", None, "space", None, None),
        ),
        out_specs=(
            P("dp", None, "space", None, None),
            P("dp", "space", None, None, None, None),
            P("space", None),
        ),
        check_vma=False,
    )
```

```python
import functools

import jax
import jax.numpy as jnp
from jax import lax
from jax.experimental import pallas as pl
from jax.experimental.pallas import tpu as pltpu
from jax.sharding import PartitionSpec as P

TPD = 16
BF = jnp.bfloat16
F32 = jnp.float32
NN = (((1,), (0,)), ((), ()))
NT = (((1,), (1,)), ((), ()))
TN = (((0,), (0,)), ((), ()))


def remote(src, dst, ssem, rsem, dev):
    return pltpu.make_async_remote_copy(
        src_ref=src,
        dst_ref=dst,
        send_sem=ssem,
        recv_sem=rsem,
        device_id=dev,
        device_id_type=pl.DeviceIdType.MESH,
    )


def loop(lo, hi, body, unroll=1):
    def step(i, carry):
        body(i)
        return carry

    lax.fori_loop(lo, hi, step, 0, unroll=unroll)


def normed(x):
    meansq = jnp.mean(x * x, axis=-1, keepdims=True)
    scale = lax.rsqrt(meansq + 1e-06)
    return x * scale, scale


def kernel(
    dims,
    owners,
    ids,
    clips_h,
    gamma,
    weight_h,
    cot_h,
    out,
    gin,
    fin,
    clips,
    weight,
    cot,
    cotprev,
    hid,
    slot_v,
    slot_s,
    stage,
    arr,
    stage2,
    ret,
    locr,
    map_v,
    map_s,
    tile32,
    tiles,
    planes,
    grads,
    gown,
    gtile32,
    xmat,
    gmat,
    cs,
    cr,
    cws,
    cwr,
    ccs,
    ccr,
    spst,
    spr,
    finr,
    in_sem,
    id_s,
    id_r,
    st_s,
    st_r,
    rt_s,
    rt_r,
    hop_s,
    hop_r,
    core_s,
    core_r,
    cw_s,
    cw_r,
    cc_s,
    cc_r,
    sp_s,
    sp_r,
    ag_s,
    ag_r,
    late_sem,
):
    ns, nx, ny, frames, half, wrows, rc, flows = dims
    spans = [(f[0][0], f[-1][1]) for f in flows]
    ndp = 2 * ny
    chans = 128
    tpd = half // 2
    me = lax.axis_index("space")
    dp = lax.axis_index("dp")
    y = dp // 2
    core = lax.rem(dp, 2)
    fj = frames * half

    def begin(k):
        return ((k * wrows) // 16) * 16

    loads = [
        pltpu.make_async_copy(clips_h, clips, in_sem.at[0]),
        pltpu.make_async_copy(cot_h, cot, in_sem.at[1]),
        pltpu.make_async_copy(weight_h, weight, in_sem.at[2]),
    ]
    for load in loads:
        load.start()
    barrier = pltpu.get_barrier_semaphore()

    def greet_space(i):
        pl.semaphore_signal(
            barrier,
            inc=1,
            device_id={"space": lax.rem(me + i, ns)},
            device_id_type=pl.DeviceIdType.MESH,
        )

    def greet_dp(sem, j, other_core):
        pl.semaphore_signal(
            sem,
            inc=1,
            device_id={"dp": 2 * j + other_core},
            device_id_type=pl.DeviceIdType.MESH,
        )

    loop(1, ny, lambda i: greet_dp(barrier, lax.rem(y + i, ny), core))

    @pl.when(core == 1)
    def _():
        loop(0, ny, lambda j: greet_dp(barrier, j, 0))

    loop(1, ns, greet_space)

    @pl.when(me == 0)
    def _():
        cotprev[...] = jnp.zeros(cotprev.shape, BF)

    @pl.when(me == ns - 1)
    def _():
        xmat[:, 6 * chans : 8 * chans] = jnp.zeros((fj, 2 * chans), BF)

    gmat[:, 27 * chans :, :] = jnp.zeros((2, gmat.shape[1] - 27 * chans, 128), F32)
    shape = (ns, 128)
    none = jnp.full((1, 128 - ids.shape[1]), tpd * ns, jnp.int32)
    id_row = jnp.concatenate([ids[...], none], axis=1)
    own_ids = jnp.broadcast_to(id_row, shape)
    first_id = lax.broadcasted_iota(jnp.int32, shape, 0) * tpd
    match = (own_ids >= first_id) & (own_ids < first_id + tpd)
    slots = lax.broadcasted_iota(jnp.int32, shape, 1)
    slot_of = jnp.max(jnp.where(match, slots, 0), axis=1, keepdims=True)
    slot_of = jnp.minimum(slot_of, clips.shape[0] - 1)
    slot_v[...] = jnp.broadcast_to(slot_of, (ns, 128))
    locr[me] = id_row
    slot_copy = pltpu.make_async_copy(slot_v, slot_s, in_sem.at[4])
    slot_copy.start()

    gam = gamma[...]
    loads[0].wait()

    gam_half = gam * 0.5

    def hide(k):
        x = clips[k].astype(F32)
        h = x * lax.rsqrt(jnp.mean(x * x, axis=-1, keepdims=True) + 1e-06) * gam_half
        hid[k] = (h + h * jnp.tanh(h)).astype(BF)

    loop(0, clips.shape[0], hide, 4)
    slot_copy.wait()

    def set_out(d):
        stage[d] = hid[slot_s[d, 0]]

    loop(0, ns, set_out, 4)
    arr[me] = stage[me]
    loads[1].wait()
    pl.semaphore_wait(barrier, ns - 1 + ny - 1 + ny * (1 - core))

    zme = me // nx
    xme = lax.rem(me, nx)
    nz = ns // nx

    def id_x(d, s):
        return remote(
            locr.at[zme * nx + s], locr.at[zme * nx + s], id_s.at[d], id_r.at[s],
            {"space": zme * nx + d},
        )

    def id_z(d, s):
        rows = locr.at[pl.ds(s * nx, nx)]
        return remote(
            rows, rows, id_s.at[nx + d], id_r.at[nx + s], {"space": d * nx + xme}
        )

    def tile_copy(d, s):
        return remote(stage.at[d], arr.at[s], st_s.at[d], st_r.at[s], {"space": d})

    for i in range(1, nx):
        id_x(lax.rem(xme + i, nx), xme).start()

    above = lax.rem(me + ns - 1, ns)
    under = lax.rem(me + 1, ns)
    cot_copy = remote(cot, cotprev, hop_s.at[0], hop_r.at[0], {"space": under})
    row_copy = remote(
        xmat.at[:, 0 : 2 * chans],
        xmat.at[:, 6 * chans : 8 * chans],
        hop_s.at[1],
        hop_r.at[1],
        {"space": above},
    )

    def send_tile(i):
        tile_copy(lax.rem(me + i, ns), me).start()

    loop(1, ns, send_tile)

    @pl.when(core == 0)
    def _():
        loop(0, ny, lambda j: greet_dp(late_sem, j, 1))

    for i in range(1, nx):
        d = lax.rem(xme + i, nx)
        id_x(d, d).wait_recv()
    for i in range(1, nz):
        id_z(lax.rem(zme + i, nz), zme).start()

    loads[2].wait()
    colrow = lax.rem(lax.broadcasted_iota(jnp.int32, (fj, chans), 0), half)

    def wpart(a, b):
        return weight[pl.ds((a * 9 + b * 3) * chans, 3 * chans), :]

    def back(source, b):
        total = lax.dot_general(source[...], wpart(2, b), NT, preferred_element_type=F32)
        for a in (1, 0):
            skip = (2 - a) * half
            part = lax.dot_general(
                source[skip:, :], wpart(a, b), NT, preferred_element_type=F32
            )
            total = total + jnp.concatenate(
                [part, jnp.zeros((skip, 3 * chans), F32)], axis=0
            )
        return total

    def put_planes(total, b):
        moved = pltpu.roll(total[:, 2 * chans :], 1, 0)
        moved = jnp.where(colrow == 0, 0.0, moved)
        grads[2 * b] = total[:, :chans] + moved
        grads[2 * b + 1] = total[:, chans : 2 * chans]

    put_planes(back(cot, 1), 1)

    def cut_tile(t, b):
        for par in range(2):
            for jj in range(2):
                gtile32[t, pl.ds(b * 4 + jj * 2 + par, frames, stride=8), :] = grads[
                    2 * b + par, pl.ds(2 * t + jj, frames, stride=half), :
                ]

    loop(0, tpd, lambda t: cut_tile(t, 1), 2)
    upper = back(cot, 0)
    gown[...] = upper

    for i in range(1, nz):
        d = lax.rem(zme + i, nz)
        id_z(d, d).wait_recv()
    every = locr[:, 0, :]
    low = me * tpd
    in_row = (every >= low) & (every < low + tpd)
    got = jnp.broadcast_to(
        jnp.max(jnp.where(in_row, every - low, -1), axis=1, keepdims=True), (ns, 128)
    )
    lane = lax.broadcasted_iota(jnp.int32, (ns, 128), 1)
    who = lax.broadcasted_iota(jnp.int32, (ns, 128), 0)
    src_of = jnp.max(jnp.where(got == lane, who, 0), axis=0, keepdims=True)
    map_v[0:ns, :] = got
    map_v[ns : ns + 8, :] = jnp.broadcast_to(src_of, (8, 128))
    to_scalar = pltpu.make_async_copy(map_v, map_s, in_sem.at[3])
    to_scalar.start()
    to_scalar.wait()

    def wait_tile(i):
        tile_copy(lax.rem(me + i, ns), lax.rem(me + i, ns)).wait_recv()

    loop(1, ns // 2, wait_tile)

    @pl.when(me < ns - 1)
    def _():
        cot_copy.start()

    loop(ns // 2, ns, wait_tile)

    def lay_tile(t):
        tile32[t] = arr[map_s[ns, t]].astype(F32)
        for b in range(2):
            for par in range(2):
                for jj in range(2):
                    planes[2 * b + par, pl.ds(2 * t + jj, frames, stride=half), :] = tile32[
                        t, pl.ds(b * 4 + jj * 2 + par, frames, stride=8), :
                    ]

    loop(0, tpd, lay_tile, 4)

    def next_col(even):
        return jnp.where(colrow == half - 1, 0.0, pltpu.roll(even, fj - 1, 0)).astype(BF)

    def put_rows(b):
        even = planes[2 * b]
        xmat[:, (3 * b) * chans : (3 * b + 1) * chans] = even.astype(BF)
        xmat[:, (3 * b + 1) * chans : (3 * b + 2) * chans] = planes[2 * b + 1].astype(BF)
        xmat[:, (3 * b + 2) * chans : (3 * b + 3) * chans] = next_col(even)

    put_rows(0)

    @pl.when(me > 0)
    def _():
        row_copy.start()

    put_rows(1)

    def weight_grad(b):
        for a in range(3):
            count = fj - (2 - a) * half
            part = lax.dot_general(
                xmat[0:count, 3 * b * chans : 3 * (b + 1) * chans],
                cot[fj - count :, :],
                TN,
                preferred_element_type=F32,
            )
            row = (9 * a + 3 * b) * chans
            gmat[0, row : row + 3 * chans, :] = part[:, :128]
            gmat[1, row : row + 3 * chans, :] = part[:, 128:]

    other = {"dp": 2 * y + 1 - core}

    def core_copy(k, f):
        lo, hi = spans[f]
        return remote(
            cs.at[k, lo:hi], cr.at[k, lo:hi], core_s.at[f, k], core_r.at[f, k], other
        )

    ups = (ny // 2, ny - 1 - ny // 2)
    downs = (ups[1], ups[0])

    def each(f, body):
        for lo, hi, shift in flows[f]:
            loop(lo, hi, lambda q, shift=shift: body(q, q + shift))

    def send_core(f):
        def pack(q, s):
            row = pl.multiple_of(begin(s), 16)
            window = gmat[1 - core, pl.ds(row, rc * ny), :].astype(BF)
            cs[:, q] = window.reshape(ny, rc, 128)

        each(f, pack)
        for i in range(max(ups[f], downs[f])):
            if i < ups[f]:
                core_copy(lax.rem(y + ups[f] - i, ny), f).start()
            if i < downs[f]:
                core_copy(lax.rem(y + ny - downs[f] + i, ny), f).start()
        core_copy(y, f).start()

    def mine(k, q, s):
        row = pl.multiple_of(begin(s) + rc * k, 16)
        return gmat[core, pl.ds(row, rc), :] + cr[k, q].astype(F32)

    up = {"dp": 2 * lax.rem(y + 1, ny) + core}
    down = {"dp": 2 * lax.rem(y + ny - 1, ny) + core}

    def up_copy(i, f, r):
        lo, hi, _ = flows[f][r]
        n = sum(len(flow) for flow in flows[:f]) + r
        return remote(cws.at[i, lo:hi], cwr.at[i, lo:hi], cw_s.at[n, i], cw_r.at[n, i], up)

    def down_copy(i, f, r):
        lo, hi, _ = flows[f][r]
        n = sum(len(flow) for flow in flows[:f]) + r
        return remote(ccs.at[i, lo:hi], ccr.at[i, lo:hi], cc_s.at[n, i], cc_r.at[n, i], down)

    def hop(k, i, f, r, send, into, out_of):
        lo, hi, shift = flows[f][r]
        if i > 0:
            send(i - 1, f, r).wait_recv()

        def add(q):
            v = mine(k, q, q + shift)
            if i > 0:
                v = v + out_of[i - 1, q].astype(F32)
            into[i, q] = v.astype(BF)

        loop(lo, hi, add, hi - lo)
        send(i, f, r).start()

    def chain(f, i):
        k_up = lax.rem(y + ups[f] - i + ny, ny)
        k_down = lax.rem(y + ny - downs[f] + i, ny)
        if i < ups[f]:
            core_copy(k_up, f).wait_recv()
        if i < downs[f]:
            core_copy(k_down, f).wait_recv()
        for r in range(len(flows[f])):
            if i < ups[f]:
                hop(k_up, i, f, r, up_copy, cws, cwr)
            if i < downs[f]:
                hop(k_down, i, f, r, down_copy, ccs, ccr)

    weight_grad(1)
    weight_grad(0)

    @pl.when(core == 1)
    def _():
        pl.semaphore_wait(late_sem, ny)

    send_core(0)
    chain(0, 0)

    @pl.when(me > 0)
    def _():
        cot_copy.wait_recv()

    put_planes(gown[...] + back(cotprev, 2), 0)

    def cut_upper(t):
        cut_tile(t, 0)
        tiles[t] = gtile32[t].astype(BF)

    loop(0, tpd, cut_upper, 4)

    def back_copy(d, s):
        return remote(stage2.at[d], ret.at[s], rt_s.at[d], rt_r.at[s], {"space": d})

    def send_back(i):
        d = lax.rem(me + i, ns)
        stage2[d] = tiles[jnp.maximum(map_s[d, 0], 0)]
        back_copy(d, me).start()

    loop(1, ns, send_back)
    ret[me] = tiles[jnp.maximum(map_s[me, 0], 0)]

    @pl.when(me < ns - 1)
    def _():
        row_copy.wait_recv()

    xmat[:, 8 * chans : 9 * chans] = next_col(
        xmat[:, 6 * chans : 7 * chans].astype(F32)
    )
    weight_grad(2)
    send_core(1)
    chain(0, 1)
    chain(1, 0)

    for i in range(2, max(ups)):
        chain(0, i)
        chain(1, i - 1)

    def sp_copy(d, s):
        return remote(spst.at[d], spr.at[s], sp_s.at[d], sp_r.at[s], {"space": d})

    def spread(f):
        core_copy(y, f).wait_recv()
        for r, (lo, hi, shift) in enumerate(flows[f]):
            for send, steps in ((up_copy, ups), (down_copy, downs)):
                if steps[f] > 0:
                    send(steps[f] - 1, f, r).wait_recv()

            def part(q, shift=shift):
                s = q + shift
                v = mine(y, q, s)
                for landed, steps in ((cwr, ups), (ccr, downs)):
                    if steps[f] > 0:
                        v = v + landed[steps[f] - 1, q].astype(F32)
                spst[s] = v.astype(BF)

                @pl.when(s != me)
                def _():
                    sp_copy(s, me).start()

            loop(lo, hi, part)

    def done_tiles(i):
        tile_copy(lax.rem(me + i, ns), me).wait_send()

    loop(1, ns, done_tiles)
    for i in range(1, nx):
        id_x(lax.rem(xme + i, nx), xme).wait_send()
    for i in range(1, nz):
        id_z(lax.rem(zme + i, nz), zme).wait_send()

    @pl.when(me < ns - 1)
    def _():
        cot_copy.wait_send()

    @pl.when(me > 0)
    def _():
        row_copy.wait_send()

    spread(0)
    chain(1, max(ups) - 1)
    spread(1)
    spr[me] = spst[me]

    def done_core(k):
        for f in range(2):
            core_copy(k, f).wait_send()

    loop(0, ny, done_core)
    for f in range(2):
        for r in range(len(flows[f])):
            for i in range(ups[f]):
                up_copy(i, f, r).wait_send()
            for i in range(downs[f]):
                down_copy(i, f, r).wait_send()

    total = lax.dot_general(xmat[...], weight[18 * chans :, :], NN, preferred_element_type=F32)
    for a in (1, 0):
        skip = (2 - a) * half
        part = lax.dot_general(
            xmat[0 : fj - skip, :],
            weight[9 * a * chans : 9 * (a + 1) * chans, :],
            NN,
            preferred_element_type=F32,
        )
        total = total + jnp.concatenate([jnp.zeros((skip, 256), F32), part], axis=0)
    out[...] = total.astype(BF)

    def wait_back(i):
        back_copy(lax.rem(me + i, ns), lax.rem(me + i, ns)).wait_recv()
        back_copy(lax.rem(me + i, ns), me).wait_send()

    loop(1, ns, wait_back)

    def pull(k):
        tile = owners[k]
        g = ret[jnp.minimum(tile // tpd, ns - 1)].astype(F32)
        g = jnp.where(tile < tpd * ns, g, 0.0)
        n, scale = normed(clips[k].astype(F32))
        v = n * gam
        sig = 0.5 + 0.5 * jnp.tanh(0.5 * v)
        dn = g * sig * (1.0 + v * (1.0 - sig)) * gam
        gin[k] = (scale * (dn - n * jnp.mean(dn * n, axis=-1, keepdims=True))).astype(BF)

    middle = clips.shape[0] // 2
    loop(0, middle, pull, 4)

    def wait_sp(i):
        sp_copy(lax.rem(me + i, ns), lax.rem(me + i, ns)).wait_recv()

    loop(1, ns, wait_sp)
    finr[core, y] = jnp.sum(spr[...].astype(F32), axis=0).astype(BF)

    def ag_copy(d, s):
        slot = finr.at[lax.rem(s, 2), s // 2]
        return remote(slot, slot, ag_s.at[d], ag_r.at[s], {"dp": d})

    def send_ag(i):
        ag_copy(lax.rem(dp + i, ndp), dp).start()

    loop(1, ndp, send_ag)

    loop(middle, clips.shape[0], pull, 4)

    def done_sp(i):
        sp_copy(lax.rem(me + i, ns), me).wait_send()

    loop(1, ns, done_sp)

    def wait_ag(i):
        d = lax.rem(dp + i, ndp)
        ag_copy(d, d).wait_recv()

    loop(1, ndp, wait_ag)
    for off in range(0, 16, 4):

        @pl.when(me * wrows - begin(me) == off)
        def _(off=off):
            for h in range(2):
                window = finr[h].reshape(ny * rc, 128).astype(F32)
                fin[:, h * 128 : (h + 1) * 128] = window[off : off + wrows]

    def done_dp(i):
        ag_copy(lax.rem(dp + i, ndp), dp).wait_send()

    loop(1, ndp, done_dp)


def pin(x):
    return pltpu.with_memory_space_constraint(x, pltpu.HBM)


def settle(out, gin, fin, out_to, gin_to, fin_to, sem):
    pairs = ((out, out_to), (gin, gin_to), (fin, fin_to))
    copies = [pltpu.make_async_copy(a, b, sem.at[i]) for i, (a, b) in enumerate(pairs)]
    for copy in copies:
        copy.start()
    for copy in copies:
        copy.wait()


def flows(ns, wrows):
    kinds = [[], []]
    for s in range(ns):
        taps = range(s * wrows // 128, (s * wrows + wrows - 1) // 128 + 1)
        kinds[1 if any((tap % 9) // 3 == 2 for tap in taps) else 0].append(s)
    found = []
    q = 0
    for kind in kinds:
        ranges = []
        for s in kind:
            if ranges and ranges[-1][1] + ranges[-1][2] == s:
                ranges[-1] = (ranges[-1][0], q + 1, ranges[-1][2])
            else:
                ranges.append((q, q + 1, s - q))
            q += 1
        found.append(tuple(ranges))
    return tuple(found)


def local(clips, a_tile, gamma, weight, cotangent):
    ns = lax.axis_size("space")
    ny = lax.axis_size("dp") // 2
    frames, rows_in, tcols, chans = clips.shape[2:]
    half = cotangent.shape[3]
    tpd = half // 2
    cap = clips.shape[1]
    fj = frames * half
    trows = frames * rows_in * tcols
    wrows = weight.shape[0] // ns
    nx = 4
    ranges = sum(len(flow) for flow in flows(ns, wrows))
    rc = 16 * -(-(wrows + 12) // (16 * ny))
    pad = max(((s * wrows) // 16) * 16 + rc * ny for s in range(ns))
    vmem = pl.BlockSpec(memory_space=pltpu.VMEM)
    smem = pl.BlockSpec(memory_space=pltpu.SMEM)
    hbm = pl.BlockSpec(memory_space=pltpu.HBM)
    dma = pltpu.SemaphoreType.DMA
    tiles_shape = pltpu.VMEM((ns, trows, chans), BF)
    reach = ny // 2
    piece = (ns, rc, 128)
    out, gin, fin = pl.pallas_call(
        functools.partial(kernel, (ns, nx, ny, frames, half, wrows, rc, flows(ns, wrows))),
        out_shape=(
            jax.ShapeDtypeStruct((fj, 256), BF),
            jax.ShapeDtypeStruct((cap, trows, chans), BF),
            jax.ShapeDtypeStruct((wrows, 256), F32),
        ),
        in_specs=[smem, vmem, hbm, vmem, hbm, hbm],
        out_specs=(vmem, vmem, vmem),
        scratch_shapes=[
            pltpu.VMEM((cap, trows, chans), BF),
            pltpu.VMEM(weight.shape, BF),
            pltpu.VMEM((fj, 256), BF),
            pltpu.VMEM((fj, 256), BF),
            pltpu.VMEM((cap, trows, chans), BF),
            pltpu.VMEM((ns, 128), jnp.int32),
            pltpu.SMEM((ns, 128), jnp.int32),
            tiles_shape,
            tiles_shape,
            tiles_shape,
            tiles_shape,
            pltpu.VMEM((ns, 1, 128), jnp.int32),
            pltpu.VMEM((ns + 8, 128), jnp.int32),
            pltpu.SMEM((ns + 8, 128), jnp.int32),
            pltpu.VMEM((tpd, trows, chans), F32),
            pltpu.VMEM((tpd, trows, chans), BF),
            pltpu.VMEM((4, fj, chans), F32),
            pltpu.VMEM((4, fj, chans), F32),
            pltpu.VMEM((fj, 3 * chans), F32),
            pltpu.VMEM((tpd, trows, chans), F32),
            pltpu.VMEM((fj, 9 * chans), BF),
            pltpu.VMEM((2, pad, 128), F32),
            pltpu.VMEM((ny,) + piece, BF),
            pltpu.VMEM((ny,) + piece, BF),
            pltpu.VMEM((reach,) + piece, BF),
            pltpu.VMEM((reach,) + piece, BF),
            pltpu.VMEM((reach,) + piece, BF),
            pltpu.VMEM((reach,) + piece, BF),
            pltpu.VMEM(piece, BF),
            pltpu.VMEM(piece, BF),
            pltpu.VMEM((2, ny, rc, 128), BF),
            dma((5,)),
            dma((nx + ns // nx,)),
            dma((nx + ns // nx,)),
            dma((ns,)),
            dma((ns,)),
            dma((ns,)),
            dma((ns,)),
            dma((2,)),
            dma((2,)),
            dma((2, ny)),
            dma((2, ny)),
            dma((ranges, reach)),
            dma((ranges, reach)),
            dma((ranges, reach)),
            dma((ranges, reach)),
            dma((ns,)),
            dma((ns,)),
            dma((2 * ny,)),
            dma((2 * ny,)),
            pltpu.SemaphoreType.REGULAR,
        ],
        compiler_params=pltpu.CompilerParams(
            collective_id=0, has_side_effects=True, vmem_limit_bytes=48 * 1024 * 1024
        ),
    )(
        pin(a_tile[0]),
        pin(a_tile),
        pin(clips.reshape(cap, trows, chans)),
        pin(gamma.reshape(1, chans)),
        pin(weight),
        pin(cotangent.reshape(fj, 256)),
    )
    any_ = pl.BlockSpec(memory_space=pl.ANY)
    out, gin, fin = pl.pallas_call(
        settle,
        out_shape=tuple(jax.ShapeDtypeStruct(v.shape, v.dtype) for v in (out, gin, fin)),
        in_specs=[vmem] * 3,
        out_specs=(any_,) * 3,
        scratch_shapes=[dma((3,))],
    )(*(pltpu.with_memory_space_constraint(v, pltpu.VMEM) for v in (out, gin, fin)))
    return (
        out.reshape(1, frames, 1, half, 256),
        gin.reshape(clips.shape),
        fin,
    )


def solution(mesh):
    return jax.shard_map(
        local,
        mesh=mesh,
        in_specs=(
            P("dp", "space", None, None, None, None),
            P("dp", "space"),
            P(),
            P(),
            P("dp", None, "space", None, None),
        ),
        out_specs=(
            P("dp", None, "space", None, None),
            P("dp", "space", None, None, None, None),
            P("space", None),
        ),
        check_vma=False,
    )
```
